32 devices in a mesh: depth: 4 (over z), gx: 2 (over y), gy: 4 (over x, core).
Axes of the slice: x: 2, y: 2, z: 4, core: 2. Of those that a mesh axis runs over, the one named last changes fastest.
Arguments:
- source: float32 [8, 2, 4, 128, 512], P('depth', None, None, 'gx', 'gy'), may hold values from -6 to 6
- observed: float32 [8, 2, 4, 128, 512], P('depth', None, None, 'gx', 'gy'), may hold values from -8 to 8
- wavenumber: float32 [8, 128, 512], P('depth', 'gx', 'gy'), may hold values from 0.5 to 1.5
- damping: float32 [8, 128, 512], P('depth', 'gx', 'gy'), may hold values from 0.5 to 2
Outputs:
- forward_field: float32 [8, 2, 4, 128, 512], P('depth', None, None, 'gx', 'gy')
- gradient: float32 [8, 128, 512], P('depth', 'gx', 'gy')
The draws below stay inside these ranges and needn't reach their ends.
All inputs are finite; a program needn't handle non-finite values.
Results may differ from the reference program's by a relative error of at most 0.00002.
Values sent between devices are 32-bit elements; how exact they have to be, the bound alone decides.
No kernel may reach another device: no remote copies, remote signals or barrier semaphores. Data moves between devices by JAX's collectives and lax.ppermute only.
A program may use at most 64 MiB of HBM per device.

```python
import math
import jax
import jax.numpy as jnp
from jax import lax

SHOTS = 4
NX = 128
NY = 512
NZ = 8


def level_of(rng, dims, split, least, top_value):
    level, own = 1.0, jax.random.fold_in(rng, 6)
    for axis_at, shards_of in split:
        steps = jnp.exp(jax.random.uniform(jax.random.fold_in(own, axis_at), (shards_of,), jnp.float32, least / len(split), top_value / len(split)))
        level = level * jnp.repeat(steps, dims[axis_at] // shards_of).reshape([-1 if axis == axis_at else 1 for axis in range(len(dims))])
    return level


def gaussian(key, shape, width, limit, pieces=(), held_as=jnp.bfloat16):
    drawn = jax.random.normal(key, shape, jnp.float32) * width
    if len(pieces) > 0:
        drawn = level_of(key, shape, pieces, -0.22, 0.18) * drawn
    return jnp.clip(drawn, min=-limit, max=limit).astype(held_as)


def setup_inputs(seed: int = 0) -> dict:
    streams_of = jax.random.split(jax.random.key(seed), 5)
    return {
        "source": gaussian(streams_of[0], (NZ, 2, SHOTS, NX, NY), 1.0, 6.0, ((0, 4), (3, 2), (4, 4)), jnp.float32),
        "observed": gaussian(streams_of[1], (NZ, 2, SHOTS, NX, NY), 2.0, 8.0, ((0, 4), (3, 2), (4, 4)), jnp.float32),
        "wavenumber": jnp.clip(0.5 + 1.0 * jax.random.uniform(streams_of[2], (NZ, NX, NY), jnp.float32) ** level_of(streams_of[2], (NZ, NX, NY), ((0, 4), (1, 2), (2, 4)), -0.2, 0.2), 0.5, 1.5),
        "damping": jnp.clip(jnp.exp(math.log(2.0) - 1.3862944 * jax.random.uniform(streams_of[3], (NZ, NX, NY), jnp.float32) ** level_of(streams_of[3], (NZ, NX, NY), ((0, 4), (1, 2), (2, 4)), -0.2, 0.2)), 0.5, 2.0),
    }


def lateral_sum(plane):
    padded = jnp.pad(plane, ((0, 0), (0, 0), (1, 1), (1, 1)))
    return padded[:, :, 2:, 1:-1] + padded[:, :, :-2, 1:-1] + padded[:, :, 1:-1, 2:] + padded[:, :, 1:-1, :-2]


def complex_scale(plane, inverse):
    real_part = inverse[0][None]
    imag_part = inverse[1][None]
    return jnp.stack([plane[0] * real_part - plane[1] * imag_part, plane[0] * imag_part + plane[1] * real_part])


def relax(drive, inverse):
    field = complex_scale(drive, inverse)
    for sweep_step in range(2):
        field = complex_scale(drive + lateral_sum(field), inverse)
    return field


def inverses(wavenumber, damping):
    real_diag = 6.0 - wavenumber
    denom = real_diag * real_diag + damping * damping
    return real_diag / denom, damping / denom


def sweep(drive, inverse, reverse):
    def advance(carry, items):
        plane, inv_plane = items
        result = relax(plane + 2.5 * carry, inv_plane)
        return result, result

    start = jnp.zeros(drive.shape[1:], jnp.float32)
    final, fields = lax.scan(advance, start, (drive, inverse), reverse=reverse)
    return fields


def reference(source, observed, wavenumber, damping):
    inv_real, inv_imag = inverses(wavenumber, damping)
    inv_fwd = jnp.stack([inv_real, -inv_imag], axis=1)
    inv_adj = jnp.stack([inv_real, inv_imag], axis=1)
    forward_field = sweep(source, inv_fwd, False)
    residual = forward_field - observed
    adjoint = sweep(residual, inv_adj, True)
    product = forward_field[:, 0] * adjoint[:, 0] + forward_field[:, 1] * adjoint[:, 1]
    gradient = jnp.mean(product, axis=1)
    return forward_field, gradient
```

```python
import jax
import jax.numpy as jnp
from jax import lax
from jax.experimental import pallas as pl
from jax.experimental.pallas import tpu as pltpu
from jax.sharding import PartitionSpec as P

MEMBERS = 4
WIDE = 32
NARROW = 16
LANES = 128

VMEM = pltpu.VMEM
F32 = jnp.float32


def lane_ids(shape):
    return lax.broadcasted_iota(jnp.int32, shape, len(shape) - 1)


def call(kernel, outs, meta, *operands, scratch=()):
    return pl.pallas_call(
        kernel,
        out_shape=[jax.ShapeDtypeStruct(shape, F32) for shape in outs],
        in_specs=[pl.BlockSpec(memory_space=pltpu.SMEM)]
        + [pl.BlockSpec(memory_space=VMEM)] * len(operands),
        out_specs=[pl.BlockSpec(memory_space=VMEM)] * len(outs),
        scratch_shapes=list(scratch),
        compiler_params=pltpu.CompilerParams(vmem_limit_bytes=48 * 1024 * 1024),
    )(meta, *operands)


def member_swap(block, offset):
    nz, nx = lax.axis_size("depth"), lax.axis_size("gx")
    dz, dx = offset >> 1, offset & 1
    pairs = [(z * nx + x, (z ^ dz) * nx + (x ^ dx)) for z in range(nz) for x in range(nx)]
    return lax.ppermute(block, ("depth", "gx"), pairs)


def depth_pair_swap(block):
    return lax.ppermute(block, "depth", [(z, z ^ 2) for z in range(lax.axis_size("depth"))])


def neighbour_swaps(first, second, axis, stride):
    size = lax.axis_size(axis)
    count = size // stride

    def pairs(start):
        found = []
        for low in range(start, count - 1, 2):
            for part in range(stride):
                a, b = low * stride + part, (low + 1) * stride + part
                found += [(a, b), (b, a)]
        return found

    got_first = lax.ppermute(first, axis, pairs(0)) if count > 1 else jnp.zeros_like(first)
    got_second = lax.ppermute(second, axis, pairs(1)) if count > 2 else jnp.zeros_like(second)
    return got_first, got_second


def with_row_halo(block, width):
    groups = lax.axis_size("gx") // 2
    if groups == 1:
        return block
    even = (lax.axis_index("gx") // 2) % 2 == 0
    top, bottom = block[..., :width, :], block[..., -width:, :]
    one, two = neighbour_swaps(
        jnp.where(even, bottom, top), jnp.where(even, top, bottom), "gx", 2
    )
    above, below = jnp.where(even, two, one), jnp.where(even, one, two)
    return jnp.concatenate([above, block, below], axis=-2)


def merge_members(meta, pieces, out):
    me = meta[0]
    for k, piece in enumerate(pieces):
        fields, planes, _, rows, _ = piece.shape
        who = me ^ k
        at_plane = (who // 2) * planes
        at_row = pl.multiple_of((who % 2) * rows, rows)
        for f in range(fields):
            for p in range(planes):
                for c in range(2):
                    out[f, at_plane + p, c, pl.ds(at_row, rows), :] = piece[f, p, c]


def pack_edges(meta, tiles, width, first, second):
    even = meta[1] == 0
    lanes = lane_ids(tiles[0].shape)
    left = right = None
    for j, tile in enumerate(tiles):
        at = j * width
        from_left = pltpu.roll(tile, at, 1) if at else tile
        turn = (at + width) % LANES
        from_right = pltpu.roll(tile, turn, 1) if turn else tile
        if left is None:
            left, right = from_left, from_right
        else:
            left = jnp.where(lanes >= at, from_left, left)
            right = jnp.where(lanes >= at, from_right, right)
    first[...] = jnp.where(even, right, left)
    second[...] = jnp.where(even, left, right)


def unpack_edges(meta, first, second, j, width):
    even = meta[1] == 0
    right, left = jnp.where(even, first, second), jnp.where(even, second, first)
    lanes = lane_ids(first.shape)
    at = j * width
    right = pltpu.roll(right, LANES - at, 1) if at else right
    turn = (LANES - width - at) % LANES
    left = pltpu.roll(left, turn, 1) if turn else left
    return jnp.where(lanes < width, right, jnp.where(lanes >= LANES - width, left, 0.0))


def pack_carry(field, at, out):
    real, imag = field[at, 0, :, LANES:], field[at, 1, :, LANES:]
    lanes = lane_ids(real.shape)
    middle = (lanes >= WIDE) & (lanes < LANES - WIDE)
    out[0] = field[at, 0, :, :LANES]
    out[1] = field[at, 1, :, :LANES]
    out[2] = jnp.where(middle, pltpu.roll(imag, LANES // 2, 1), real)


def unpack_carry(packed, use, out):
    edges = packed[2]
    lanes = lane_ids(edges.shape)
    middle = (lanes >= WIDE) & (lanes < LANES - WIDE)
    keep = use & jnp.logical_not(middle)
    for c in range(2):
        out[c, :, :LANES] = jnp.where(use, packed[c], 0.0)
        out[c, :, LANES:] = jnp.where(keep, pltpu.roll(edges, LANES // 2, 1) if c else edges, 0.0)


def times(a, b, q_real, q_imag, sign):
    if sign > 0:
        return a * q_real - b * q_imag, a * q_imag + b * q_real
    return a * q_real + b * q_imag, b * q_real - a * q_imag


def sweep(drive, inverse, out, carry, work, planes, rows, reverse):
    rhs, ping, pong = work
    sign = -1 if reverse else 1
    zeros = jnp.zeros((8, 2 * LANES), F32)
    for buffer in (ping, pong):
        for c in range(2):
            buffer[c, :8, :] = zeros
            buffer[c, rows + 8 : rows + 16, :] = zeros

    def beside(buffer, c, r):
        here = buffer[c, r + 8 : r + 16, :]
        return (
            buffer[c, r + 7 : r + 15, :]
            + buffer[c, r + 9 : r + 17, :]
            + (pltpu.roll(here, 1, 1) + pltpu.roll(here, 2 * LANES - 1, 1))
        )

    def plane(step, _):
        z = planes - 1 - step if reverse else step
        for r in range(0, rows, 8):
            strip = slice(r, r + 8)
            a = drive[z, 0, strip, :] + 2.5 * carry[0, strip, :]
            b = drive[z, 1, strip, :] + 2.5 * carry[1, strip, :]
            rhs[0, strip, :] = a
            rhs[1, strip, :] = b
            a, b = times(a, b, inverse[z, 0, strip, :], inverse[z, 1, strip, :], sign)
            ping[0, r + 8 : r + 16, :] = a
            ping[1, r + 8 : r + 16, :] = b
        for r in range(0, rows, 8):
            strip = slice(r, r + 8)
            a = rhs[0, strip, :] + beside(ping, 0, r)
            b = rhs[1, strip, :] + beside(ping, 1, r)
            a, b = times(a, b, inverse[z, 0, strip, :], inverse[z, 1, strip, :], sign)
            pong[0, r + 8 : r + 16, :] = a
            pong[1, r + 8 : r + 16, :] = b
        for r in range(0, rows, 8):
            strip = slice(r, r + 8)
            a = rhs[0, strip, :] + beside(pong, 0, r)
            b = rhs[1, strip, :] + beside(pong, 1, r)
            a, b = times(a, b, inverse[z, 0, strip, :], inverse[z, 1, strip, :], sign)
            out[z, 0, strip, :] = a
            out[z, 1, strip, :] = b
            carry[0, strip, :] = a
            carry[1, strip, :] = b
        return 0

    lax.fori_loop(0, planes, plane, 0)


def sweep_scratch(rows):
    wide = 2 * LANES
    return [
        VMEM((2, rows, wide), F32),
        VMEM((2, rows, wide), F32),
        VMEM((2, rows + 16, wide), F32),
        VMEM((2, rows + 16, wide), F32),
    ]


def prepare_kernel(meta, source, wavenumber, damping, *sends):
    real_diag = 6.0 - wavenumber[...]
    damp = damping[...]
    denom = real_diag * real_diag + damp * damp
    real = real_diag / denom
    imag = -(damp / denom)
    for k, send in enumerate(sends):
        send[0] = source[:, :, meta[0] ^ k]
        send[1, :, 0] = real
        send[1, :, 1] = imag


def prepare_observed_kernel(meta, observed, *sends):
    for k, send in enumerate(sends):
        send[0] = observed[:, :, meta[0] ^ k]


def merge_kernel(meta, *refs):
    merge_members(meta, refs[:MEMBERS], refs[MEMBERS])


def pack_wide(meta, merged, first, second):
    for f in range(2):
        for c in range(2):
            tiles = [merged[f, p, c] for p in range(merged.shape[1])]
            pack_edges(meta, tiles, WIDE, first.at[f, c], second.at[f, c])


def pack_narrow(meta, merged, first, second):
    tiles = [merged[0, p, c] for p in range(merged.shape[1]) for c in range(2)]
    pack_edges(meta, tiles, NARROW, first, second)


def widen(merged, edges, outs):
    for f, out in enumerate(outs):
        for p in range(merged.shape[1]):
            for c in range(2):
                out[p, c, :, :LANES] = merged[f, p, c]
                out[p, c, :, LANES:] = edges(f, p, c)


def forward_kernel(meta, merged, first, second, drive, inverse, send, field, carry, *work):
    planes, rows = merged.shape[1], merged.shape[3]
    widen(
        merged,
        lambda f, p, c: unpack_edges(meta, first[f, c], second[f, c], p, WIDE),
        (drive, inverse),
    )
    carry[...] = jnp.zeros_like(carry)
    sweep(drive, inverse, field, carry, work, planes, rows, False)
    pack_carry(field, planes - 1, send)


def turn_kernel(
    height, meta, drive, inverse, got, observed, first, second, field, residual, send, *rest
):
    pieces, (adjoint, carry, *work) = rest[:MEMBERS], rest[MEMBERS:]
    planes, rows = drive.shape[0], drive.shape[2]
    margin = (rows - 2 * height) // 2
    unpack_carry(got, meta[2] == 1, carry)
    sweep(drive, inverse, field, carry, work, planes, rows, False)
    for p in range(planes):
        for c in range(2):
            edges = unpack_edges(meta, first[...], second[...], 2 * p + c, NARROW)
            residual[p, c, :, :LANES] = field[p, c, :, :LANES] - observed[0, p, c]
            residual[p, c, :, LANES:] = field[p, c, :, LANES:] - edges
    carry[...] = jnp.zeros_like(carry)
    sweep(residual, inverse, adjoint, carry, work, planes, rows, True)
    pack_carry(adjoint, 0, send)
    for k, piece in enumerate(pieces):
        who = meta[0] ^ k
        at_plane = (who // 2) * (planes // 2)
        at_row = pl.multiple_of((who % 2) * height + margin, 8)
        for p in range(planes // 2):
            for c in range(2):
                piece[p, c] = field[at_plane + p, c, pl.ds(at_row, height), :LANES]


def adjoint_kernel(height, meta, residual, inverse, got, field, *rest):
    pieces, (adjoint, carry, *work) = rest[:MEMBERS], rest[MEMBERS:]
    planes, rows = residual.shape[0], residual.shape[2]
    margin = (rows - 2 * height) // 2
    unpack_carry(got, meta[2] == 0, carry)
    sweep(residual, inverse, adjoint, carry, work, planes, rows, True)
    for k, piece in enumerate(pieces):
        who = meta[0] ^ k
        at_plane = (who // 2) * (planes // 2)
        at_row = pl.multiple_of((who % 2) * height + margin, 8)
        for p in range(planes // 2):
            total = 0.0
            for c in range(2):
                total += (
                    field[at_plane + p, c, pl.ds(at_row, height), :LANES]
                    * adjoint[at_plane + p, c, pl.ds(at_row, height), :LANES]
                )
            piece[p] = total * (1.0 / MEMBERS)


def field_kernel(meta, *refs):
    out = refs[MEMBERS]
    for k, piece in enumerate(refs[:MEMBERS]):
        out[:, :, meta[0] ^ k] = piece[...]


def body(source, observed, wavenumber, damping):
    own_planes, _, shots, height, width = source.shape
    zi, xi, yi = (lax.axis_index(a) for a in ("depth", "gx", "gy"))
    meta = jnp.stack([2 * (zi % 2) + xi % 2, yi % 2, zi // 2]).astype(jnp.int32)
    planes, high = 2 * own_planes, 2 * height
    one_group = lax.axis_size("gx") == 2
    rows = high if one_group else high + 2 * WIDE
    tile = (own_planes, 2, height, width)
    all_ks = range(1, MEMBERS)

    def gathered(sends, fields, pack, edge_shape):
        pieces = [sends[0]] + [member_swap(sends[k], k) for k in all_ks]
        merged_shape = (fields, planes, 2, high, width)
        if one_group:

            def merge_pack(meta, *refs):
                merge_members(meta, refs[:MEMBERS], refs[MEMBERS])
                pack(meta, *refs[MEMBERS:])

            merged, first, second = call(
                merge_pack, [merged_shape, edge_shape, edge_shape], meta, *pieces
            )
        else:
            merged = with_row_halo(call(merge_kernel, [merged_shape], meta, *pieces)[0], WIDE)
            first, second = call(pack, [edge_shape, edge_shape], meta, merged)
        return merged, *neighbour_swaps(first, second, "gy", 1)

    sends = call(prepare_kernel, [(2, *tile)] * MEMBERS, meta, source, wavenumber, damping)
    merged, first, second = gathered(sends, 2, pack_wide, (2, 2, rows, width))
    seen_sends = call(prepare_observed_kernel, [(1, *tile)] * MEMBERS, meta, observed)
    seen, seen_first, seen_second = gathered(seen_sends, 1, pack_narrow, (rows, width))

    whole = (planes, 2, rows, 2 * width)
    packed = (3, rows, width)
    drive, inverse, send = call(
        forward_kernel,
        [whole, whole, packed],
        meta,
        merged,
        first,
        second,
        scratch=[VMEM(whole, F32), *sweep_scratch(rows)],
    )
    got = depth_pair_swap(send)
    field, residual, send, *pieces = call(
        lambda *refs: turn_kernel(height, *refs),
        [whole, whole, packed] + [tile] * MEMBERS,
        meta,
        drive,
        inverse,
        got,
        seen,
        seen_first,
        seen_second,
        scratch=[VMEM(whole, F32), *sweep_scratch(rows)],
    )
    got = depth_pair_swap(send)
    pieces = [pieces[0]] + [member_swap(pieces[k], k) for k in all_ks]
    sums = call(
        lambda *refs: adjoint_kernel(height, *refs),
        [(own_planes, height, width)] * MEMBERS,
        meta,
        residual,
        inverse,
        got,
        field,
        scratch=[VMEM(whole, F32), *sweep_scratch(rows)],
    )
    gradient = sums[0]
    for k in all_ks:
        gradient = gradient + member_swap(sums[k], k)
    (forward_field,) = call(field_kernel, [source.shape], meta, *pieces)
    return forward_field, gradient


def solution(mesh):
    lateral = P("depth", None, None, "gx", "gy")
    return jax.shard_map(
        body,
        mesh=mesh,
        in_specs=(lateral, lateral, P("depth", "gx", "gy"), P("depth", "gx", "gy")),
        out_specs=(lateral, P("depth", "gx", "gy")),
        check_vma=False,
    )
```

```python
import jax
import jax.numpy as jnp
from jax import lax
from jax.experimental import pallas as pl
from jax.experimental.pallas import tpu as pltpu
from jax.sharding import PartitionSpec as P

MEMBERS = 4
WIDE = 32
NARROW = 16
LANES = 128

VMEM = pltpu.VMEM
F32 = jnp.float32


def lane_ids(shape):
    return lax.broadcasted_iota(jnp.int32, shape, len(shape) - 1)


def call(kernel, outs, meta, *operands, scratch=(), vmem=8):
    return pl.pallas_call(
        kernel,
        out_shape=[jax.ShapeDtypeStruct(shape, F32) for shape in outs],
        in_specs=[pl.BlockSpec(memory_space=pltpu.SMEM)]
        + [pl.BlockSpec(memory_space=VMEM)] * len(operands),
        out_specs=[pl.BlockSpec(memory_space=VMEM)] * len(outs),
        scratch_shapes=list(scratch),
        compiler_params=pltpu.CompilerParams(vmem_limit_bytes=vmem * 1024 * 1024),
    )(meta, *operands)


def member_swap(block, offset):
    nz, nx = lax.axis_size("depth"), lax.axis_size("gx")
    dz, dx = offset >> 1, offset & 1
    pairs = [(z * nx + x, (z ^ dz) * nx + (x ^ dx)) for z in range(nz) for x in range(nx)]
    return lax.ppermute(block, ("depth", "gx"), pairs)


def gathered(sends):
    return [sends[0]] + [member_swap(sends[k], k) for k in range(1, MEMBERS)]


def depth_pair_swap(block):
    return lax.ppermute(block, "depth", [(z, z ^ 2) for z in range(lax.axis_size("depth"))])


def neighbour_swaps(first, second, axis, stride):
    size = lax.axis_size(axis)
    count = size // stride

    def pairs(start):
        found = []
        for low in range(start, count - 1, 2):
            for part in range(stride):
                a, b = low * stride + part, (low + 1) * stride + part
                found += [(a, b), (b, a)]
        return found

    got_second = lax.ppermute(second, axis, pairs(1)) if count > 2 else jnp.zeros_like(second)
    got_first = lax.ppermute(first, axis, pairs(0)) if count > 1 else jnp.zeros_like(first)
    return got_first, got_second


def with_row_halo(block, width):
    groups = lax.axis_size("gx") // 2
    if groups == 1:
        return block
    even = (lax.axis_index("gx") // 2) % 2 == 0
    top, bottom = block[..., :width, :], block[..., -width:, :]
    one, two = neighbour_swaps(
        jnp.where(even, bottom, top), jnp.where(even, top, bottom), "gx", 2
    )
    above, below = jnp.where(even, two, one), jnp.where(even, one, two)
    return jnp.concatenate([above, block, below], axis=-2)


def merge_members(meta, pieces, out):
    me = meta[0]
    for k, piece in enumerate(pieces):
        fields, planes, _, rows, _ = piece.shape
        who = me ^ k
        at_plane = (who // 2) * planes
        at_row = pl.multiple_of((who % 2) * rows, rows)
        for f in range(fields):
            for p in range(planes):
                for c in range(2):
                    out[f, at_plane + p, c, pl.ds(at_row, rows), :] = piece[f, p, c]


def pack_edges(meta, pieces, width, first, out):
    me = meta[0]
    right = (meta[1] == 0) == first
    fields, planes, _, rows, count = pieces[0].shape
    lanes = lane_ids((rows, count))
    at = jnp.where(right, 0, width)
    second_plane = (lanes >= at) & (lanes < at + width)
    half = planes * width
    for k in range(2):
        who = me ^ k
        strip = pl.ds(pl.multiple_of((who % 2) * rows, rows), rows)
        at_lane = (who // 2) * half
        ours = (lanes >= at_lane) & (lanes < at_lane + half)
        turn = at_lane + jnp.where(right, width, 0)
        turns = turn, lax.rem(turn + half, count)
        for f in range(fields):
            for c in range(2):
                one, two = (
                    pltpu.roll(
                        jnp.where(
                            second_plane,
                            pltpu.roll(pieces[k + 2 * i][f, 1, c], width, 1),
                            pieces[k + 2 * i][f, 0, c],
                        ),
                        turns[i],
                        1,
                    )
                    for i in range(2)
                )
                out[f, c, strip, :] = jnp.where(ours, one, two)


def unpack_edges(meta, first, second, j, width):
    even = meta[1] == 0
    right, left = jnp.where(even, first, second), jnp.where(even, second, first)
    at = j * width
    return beside_tile(right, (LANES - at) % LANES, left, (LANES - width - at) % LANES, width)


def beside_tile(right, right_turn, left, left_turn, width):
    lanes = lane_ids(right.shape)
    right = pltpu.roll(right, right_turn, 1) if right_turn else right
    left = pltpu.roll(left, left_turn, 1) if left_turn else left
    return jnp.where(lanes < width, right, jnp.where(lanes >= LANES - width, left, 0.0))


def edge_lanes(shape, margin):
    lanes = lane_ids(shape)
    return (lanes < margin) | (lanes >= LANES - margin)


def slot_lanes(shape, block):
    return lax.rem(lane_ids(shape) + (LANES - 16 * block - LANES // 2 + 8), LANES // 2) < 16


def pack_carry(field, at, out, margin):
    rows = field.shape[2]
    real, imag = field[at, 0, :, LANES:], field[at, 1, :, LANES:]
    out[:rows] = field[at, 0, :, :LANES]
    out[rows : 2 * rows] = field[at, 1, :, :LANES]
    edges = jnp.where(edge_lanes(real.shape, WIDE), real, pltpu.roll(imag, LANES // 2, 1))
    if margin > 8:
        out[2 * rows :] = edges
        return
    part = rows // 4
    packed = edges[:part]
    for b in range(1, 4):
        turned = pltpu.roll(edges[b * part : (b + 1) * part], 16 * b, 1)
        packed = jnp.where(slot_lanes(packed.shape, b), turned, packed)
    out[2 * rows :] = packed


def unpack_carry(packed, use, out, margin):
    rows = out.shape[1]
    if margin > 8:
        edges = packed[2 * rows :]
    else:
        quarter = packed[2 * rows :]
        edges = jnp.concatenate(
            [pltpu.roll(quarter, LANES - 16 * b, 1) if b else quarter for b in range(4)], axis=0
        )
    keep = use & edge_lanes(edges.shape, WIDE if margin > 8 else 8)
    for c in range(2):
        out[c, :, :LANES] = jnp.where(use, packed[c * rows : (c + 1) * rows], 0.0)
        out[c, :, LANES:] = jnp.where(keep, pltpu.roll(edges, LANES // 2, 1) if c else edges, 0.0)


def times(a, b, q_real, q_imag, sign):
    if sign > 0:
        return a * q_real - b * q_imag, a * q_imag + b * q_real
    return a * q_real + b * q_imag, b * q_real - a * q_imag


def sweep(drive, inverse, out, carry, work, planes, rows, reverse):
    rhs, ping, pong = work
    sign = -1 if reverse else 1
    zeros = jnp.zeros((8, 2 * LANES), F32)
    for buffer in (ping, pong):
        for c in range(2):
            buffer[c, :8, :] = zeros
            buffer[c, rows + 8 : rows + 16, :] = zeros

    def beside(buffer, c, r):
        here = buffer[c, r + 8 : r + 16, :]
        return (
            buffer[c, r + 7 : r + 15, :]
            + buffer[c, r + 9 : r + 17, :]
            + (pltpu.roll(here, 1, 1) + pltpu.roll(here, 2 * LANES - 1, 1))
        )

    def plane(step, _):
        z = planes - 1 - step if reverse else step
        for r in range(0, rows, 8):
            strip = slice(r, r + 8)
            a = drive[z, 0, strip, :] + 2.5 * carry[0, strip, :]
            b = drive[z, 1, strip, :] + 2.5 * carry[1, strip, :]
            rhs[0, strip, :] = a
            rhs[1, strip, :] = b
            a, b = times(a, b, inverse[z, 0, strip, :], inverse[z, 1, strip, :], sign)
            ping[0, r + 8 : r + 16, :] = a
            ping[1, r + 8 : r + 16, :] = b
        for r in range(0, rows, 8):
            strip = slice(r, r + 8)
            a = rhs[0, strip, :] + beside(ping, 0, r)
            b = rhs[1, strip, :] + beside(ping, 1, r)
            a, b = times(a, b, inverse[z, 0, strip, :], inverse[z, 1, strip, :], sign)
            pong[0, r + 8 : r + 16, :] = a
            pong[1, r + 8 : r + 16, :] = b
        for r in range(0, rows, 8):
            strip = slice(r, r + 8)
            a = rhs[0, strip, :] + beside(pong, 0, r)
            b = rhs[1, strip, :] + beside(pong, 1, r)
            a, b = times(a, b, inverse[z, 0, strip, :], inverse[z, 1, strip, :], sign)
            out[z, 0, strip, :] = a
            out[z, 1, strip, :] = b
            carry[0, strip, :] = a
            carry[1, strip, :] = b
        return 0

    lax.fori_loop(0, planes, plane, 0)


def sweep_scratch(rows):
    wide = 2 * LANES
    return [
        VMEM((2, rows, wide), F32),
        VMEM((2, rows, wide), F32),
        VMEM((2, rows + 16, wide), F32),
        VMEM((2, rows + 16, wide), F32),
    ]


def inverses(wavenumber, damping):
    real_diag = 6.0 - wavenumber
    denom = real_diag * real_diag + damping * damping
    return jnp.stack([real_diag / denom, -(damping / denom)], axis=1)


def second_edges_kernel(meta, *refs):
    pack_edges(meta, refs[:MEMBERS], WIDE, False, refs[MEMBERS])


def merge_kernel(meta, *refs):
    pieces, (_, merged, out) = refs[:MEMBERS], refs[MEMBERS:]
    pack_edges(meta, pieces, WIDE, True, out)
    merge_members(meta, pieces, merged)


def observed_edges_kernel(meta, observed, first, second):
    even = meta[1] == 0
    planes, _, shots, rows, count = observed.shape
    lanes = lane_ids((rows, count))
    per_tile = count // NARROW
    sides = {}
    for s in range(shots):
        for p in range(planes):
            for c in range(2):
                tile, j = divmod((s * planes + p) * 2 + c, per_tile)
                at = j * NARROW
                block = observed[p, c, s]
                for side, turn in (("left", at), ("right", (at + NARROW) % count)):
                    got = pltpu.roll(block, turn, 1) if turn else block
                    if j:
                        got = jnp.where(lanes >= at, got, sides[side])
                    sides[side] = got
                if j == per_tile - 1:
                    first[tile] = jnp.where(even, sides["right"], sides["left"])
                    second[tile] = jnp.where(even, sides["left"], sides["right"])


def observed_sends_kernel(meta, observed, first, second, *sends):
    even = meta[1] == 0
    planes, _, _, rows, count = observed.shape
    lanes = lane_ids((rows, count))
    for k, send in enumerate(sends):
        shot = meta[0] ^ k
        for p in range(planes):
            for c in range(2):
                send[2 * p + c] = observed[p, c, shot]
        one, two = first[shot // 2], second[shot // 2]
        right, left = jnp.where(even, one, two), jnp.where(even, two, one)
        odd = lax.rem(shot, 2)
        right = pltpu.roll(right, odd * (count // 2), 1)
        left = pltpu.roll(left, (1 - odd) * (count // 2), 1)
        send[2 * planes] = jnp.where(lanes < count // 2, right, left)


def merge_observed_kernel(meta, *refs):
    pieces, out = refs[:MEMBERS], refs[MEMBERS]
    planes = out.shape[0] // 2
    _, rows, count = pieces[0].shape
    for k, piece in enumerate(pieces):
        who = meta[0] ^ k
        at_plane = (who // 2) * planes
        strip = pl.ds(pl.multiple_of((who % 2) * rows, rows), rows)
        edges = piece[2 * planes]
        for p in range(planes):
            for c in range(2):
                at = (2 * p + c) * NARROW
                out[at_plane + p, c, strip, :LANES] = piece[2 * p + c]
                out[at_plane + p, c, strip, LANES:] = beside_tile(
                    edges,
                    (count - at) % count,
                    edges,
                    (count // 2 - NARROW - at) % count,
                    NARROW,
                )


def widen(merged, edges, outs):
    for f, out in enumerate(outs):
        for p in range(merged.shape[1]):
            for c in range(2):
                out[p, c, :, :LANES] = merged[f, p, c]
                out[p, c, :, LANES:] = edges(f, p, c)


def cut_pieces(meta, field, height, pieces):
    planes, rows = field.shape[0], field.shape[2]
    margin = (rows - 2 * height) // 2
    for k, piece in enumerate(pieces):
        who = meta[0] ^ k
        at_plane = (who // 2) * (planes // 2)
        at_row = pl.multiple_of((who % 2) * height + margin, 8)
        for p in range(planes // 2):
            for c in range(2):
                piece[p, c] = field[at_plane + p, c, pl.ds(at_row, height), :LANES]


def forward_kernel(meta, merged, second, first, drive, inverse, field, send, *rest):
    carry, *work = rest
    planes, rows = merged.shape[1], merged.shape[3]
    widen(
        merged,
        lambda f, p, c: unpack_edges(meta, first[f, c], second[f, c], p, WIDE),
        (drive, inverse),
    )

    @pl.when(meta[2] == 0)
    def _():
        carry[...] = jnp.zeros_like(carry)
        sweep(drive, inverse, field, carry, work, planes, rows, False)
        pack_carry(field, planes - 1, send, WIDE)


def turn_kernel(
    height,
    meta,
    drive,
    inverse,
    got,
    observed,
    upper_field,
    field,
    residual,
    adjoint,
    send,
    *rest,
):
    pieces, (carry, *work) = rest[:MEMBERS], rest[MEMBERS:]
    planes, rows = drive.shape[0], drive.shape[2]
    lower = meta[2] == 1

    @pl.when(jnp.logical_not(lower))
    def _():
        field[...] = upper_field[...]

    @pl.when(lower)
    def _():
        unpack_carry(got, lower, carry, WIDE)
        sweep(drive, inverse, field, carry, work, planes, rows, False)

    residual[...] = field[...] - observed[...]

    @pl.when(lower)
    def _():
        carry[...] = jnp.zeros_like(carry)
        sweep(residual, inverse, adjoint, carry, work, planes, rows, True)
        pack_carry(adjoint, 0, send, 8)

    cut_pieces(meta, field, height, pieces)


def adjoint_kernel(height, meta, residual, inverse, got, field, lower_adjoint, *rest):
    pieces, (adjoint, carry, *work) = rest[:MEMBERS], rest[MEMBERS:]
    planes, rows = residual.shape[0], residual.shape[2]
    margin = (rows - 2 * height) // 2
    upper = meta[2] == 0

    def products(adjoint):
        for k, piece in enumerate(pieces):
            who = meta[0] ^ k
            at_plane = (who // 2) * (planes // 2)
            at_row = pl.multiple_of((who % 2) * height + margin, 8)
            for p in range(planes // 2):
                total = 0.0
                for c in range(2):
                    total += (
                        field[at_plane + p, c, pl.ds(at_row, height), :LANES]
                        * adjoint[at_plane + p, c, pl.ds(at_row, height), :LANES]
                    )
                piece[p] = total * (1.0 / MEMBERS)

    @pl.when(upper)
    def _():
        unpack_carry(got, upper, carry, 8)
        sweep(residual, inverse, adjoint, carry, work, planes, rows, True)
        products(adjoint)

    @pl.when(jnp.logical_not(upper))
    def _():
        products(lower_adjoint)


def field_kernel(meta, *refs):
    out = refs[MEMBERS]
    for k, piece in enumerate(refs[:MEMBERS]):
        out[:, :, meta[0] ^ k] = piece[...]


def body(source, observed, wavenumber, damping):
    own_planes, _, shots, height, width = source.shape
    zi, xi, yi = (lax.axis_index(a) for a in ("depth", "gx", "gy"))
    meta = jnp.stack([2 * (zi % 2) + xi % 2, yi % 2, zi // 2]).astype(jnp.int32)
    planes, high = 2 * own_planes, 2 * height
    one_group = lax.axis_size("gx") == 2
    rows = high if one_group else high + 2 * WIDE
    tile = (own_planes, 2, height, width)

    inverse = inverses(wavenumber, damping)
    sends = [
        jnp.stack([lax.dynamic_index_in_dim(source, meta[0] ^ k, 2, keepdims=False), inverse])
        for k in range(MEMBERS)
    ]
    observed, *sends = lax.optimization_barrier([observed, *sends])
    pieces = gathered(sends)
    seen_edges = call(observed_edges_kernel, [(2, height, width)] * 2, meta, observed)
    seen_edges = neighbour_swaps(*seen_edges, "gy", 1)
    *pieces, first, second = lax.optimization_barrier([*pieces, *seen_edges])
    seen_edges = first, second
    edge_shape = (2, 2, high, width)
    (second,) = call(second_edges_kernel, [edge_shape], meta, *pieces)
    merged, first = call(
        merge_kernel, [(2, planes, 2, high, width), edge_shape], meta, *pieces, second
    )
    if not one_group:
        merged, first, second = (with_row_halo(a, WIDE) for a in (merged, first, second))
    first, second = neighbour_swaps(first, second, "gy", 1)
    seen = gathered(
        call(
            observed_sends_kernel,
            [(2 * own_planes + 1, height, width)] * MEMBERS,
            meta,
            observed,
            *seen_edges,
        )
    )

    whole = (planes, 2, rows, 2 * width)
    scratch = sweep_scratch(rows)
    drive, inverse, field, send = call(
        forward_kernel,
        [whole, whole, whole, (3 * rows, width)],
        meta,
        merged,
        second,
        first,
        scratch=scratch,
    )
    got = depth_pair_swap(send)
    (seen,) = call(merge_observed_kernel, [(planes, 2, high, 2 * width)], meta, *seen)
    seen = seen if one_group else with_row_halo(seen, WIDE)
    field, residual, adjoint, send, *pieces = call(
        lambda *refs: turn_kernel(height, *refs),
        [whole, whole, whole, (2 * rows + rows // 4, width)] + [tile] * MEMBERS,
        meta,
        drive,
        inverse,
        got,
        seen,
        field,
        scratch=scratch,
    )
    got = depth_pair_swap(send)
    pieces = gathered(pieces)
    sums = call(
        lambda *refs: adjoint_kernel(height, *refs),
        [(own_planes, height, width)] * MEMBERS,
        meta,
        residual,
        inverse,
        got,
        field,
        adjoint,
        scratch=[VMEM(whole, F32), *scratch],
    )
    sums = gathered(sums)
    gradient = (sums[0] + sums[1]) + (sums[2] + sums[3])
    (forward_field,) = call(field_kernel, [source.shape], meta, *pieces)
    return forward_field, gradient


def solution(mesh):
    lateral = P("depth", None, None, "gx", "gy")
    return jax.shard_map(
        body,
        mesh=mesh,
        in_specs=(lateral, lateral, P("depth", "gx", "gy"), P("depth", "gx", "gy")),
        out_specs=(lateral, P("depth", "gx", "gy")),
        check_vma=False,
    )
```

```python
import jax
import jax.numpy as jnp
from jax import lax
from jax.experimental import pallas as pl
from jax.experimental.pallas import tpu as pltpu
from jax.sharding import PartitionSpec as P

MEMBERS = 4
WIDE = 32
NARROW = 16
LANES = 128
REACH = 8
DOWN = 24

VMEM = pltpu.VMEM
F32 = jnp.float32


def lane_ids(shape):
    return lax.broadcasted_iota(jnp.int32, shape, len(shape) - 1)


def call(kernel, outs, meta, *operands, scratch=(), cost=3_000_000):
    return pl.pallas_call(
        kernel,
        out_shape=[jax.ShapeDtypeStruct(shape, F32) for shape in outs],
        in_specs=[pl.BlockSpec(memory_space=pltpu.SMEM)]
        + [pl.BlockSpec(memory_space=VMEM)] * len(operands),
        out_specs=[pl.BlockSpec(memory_space=VMEM)] * len(outs),
        scratch_shapes=list(scratch),
        cost_estimate=pl.CostEstimate(flops=0, bytes_accessed=cost, transcendentals=0),
        compiler_params=pltpu.CompilerParams(vmem_limit_bytes=8 * 1024 * 1024),
    )(meta, *operands)


def member_swap(block, offset):
    nz, nx = lax.axis_size("depth"), lax.axis_size("gx")
    dz, dx = offset >> 1, offset & 1
    pairs = [(z * nx + x, (z ^ dz) * nx + (x ^ dx)) for z in range(nz) for x in range(nx)]
    return lax.ppermute(block, ("depth", "gx"), pairs)


def gathered(sends):
    return [sends[0]] + [member_swap(sends[k], k) for k in range(1, MEMBERS)]


def depth_pair_swap(block):
    return lax.ppermute(block, "depth", [(z, z ^ 2) for z in range(lax.axis_size("depth"))])


def neighbour_swaps(first, second, axis, stride, ring=False):
    size = lax.axis_size(axis)
    count = size // stride

    def pairs(start):
        found = []
        for low in range(start, count - 1, 2):
            for part in range(stride):
                a, b = low * stride + part, (low + 1) * stride + part
                found += [(a, b), (b, a)]
        return found

    ends = [(i, size - stride + i) for i in range(stride)] if ring and count % 2 == 0 else []
    ends += [(b, a) for a, b in ends]
    got_second = lax.ppermute(second, axis, pairs(1) + ends) if count > 2 else jnp.zeros_like(second)
    got_first = lax.ppermute(first, axis, pairs(0)) if count > 1 else jnp.zeros_like(first)
    return got_first, got_second


def with_row_halo(block, width):
    groups = lax.axis_size("gx") // 2
    if groups == 1:
        return block
    even = (lax.axis_index("gx") // 2) % 2 == 0
    top, bottom = block[..., :width, :], block[..., -width:, :]
    one, two = neighbour_swaps(
        jnp.where(even, bottom, top), jnp.where(even, top, bottom), "gx", 2
    )
    above, below = jnp.where(even, two, one), jnp.where(even, one, two)
    return jnp.concatenate([above, block, below], axis=-2)


def merge_members(meta, pieces, out):
    me = meta[0]
    for k, piece in enumerate(pieces):
        fields, planes, _, rows, _ = piece.shape
        who = me ^ k
        at_plane = (who // 2) * planes
        at_row = pl.multiple_of((who % 2) * rows, rows)
        for f in range(fields):
            for p in range(planes):
                for c in range(2):
                    out[f, at_plane + p, c, pl.ds(at_row, rows), :] = piece[f, p, c]


def pack_edges(meta, pieces, width, first, out):
    me, even = meta[0], meta[1] == 0
    fields, planes, _, rows, count = pieces[0].shape
    lanes = lane_ids((rows, count))

    def pack(lower, right):
        for k in range(2):
            strip = pl.ds(pl.multiple_of(((me ^ k) % 2) * rows, rows), rows)
            pair = (pieces[k + 2], pieces[k]) if lower else (pieces[k], pieces[k + 2])
            for f in range(fields):
                for c in range(2):
                    side = None
                    for j in range(2 * planes):
                        got = pair[j // planes][f, j % planes, c]
                        turn = (j * width + (width if right else 0)) % count
                        got = pltpu.roll(got, turn, 1) if turn else got
                        side = got if j == 0 else jnp.where(lanes >= j * width, got, side)
                    out[f, c, strip, :] = side

    for lower in (False, True):
        for right in (False, True):
            pl.when(((me >= 2) == lower) & ((even == first) == right))(
                lambda lower=lower, right=right: pack(lower, right)
            )


def unpack_edges(meta, first, second, j, width):
    even = meta[1] == 0
    right, left = jnp.where(even, first, second), jnp.where(even, second, first)
    at = j * width
    return beside_tile(right, (LANES - at) % LANES, left, (LANES - width - at) % LANES, width)


def beside_tile(right, right_turn, left, left_turn, width):
    lanes = lane_ids(right.shape)
    right = pltpu.roll(right, right_turn, 1) if right_turn else right
    left = pltpu.roll(left, left_turn, 1) if left_turn else left
    return jnp.where(lanes < width, right, jnp.where(lanes >= LANES - width, left, 0.0))


def edge_lanes(shape, margin):
    lanes = lane_ids(shape)
    return (lanes < margin) | (lanes >= LANES - margin)


def slot_lanes(shape, block):
    return lax.rem(lane_ids(shape) + (LANES - 16 * block - LANES // 2 + 8), LANES // 2) < 16


def folded_edges(field, at):
    real, imag = field[at, 0, :, LANES:], field[at, 1, :, LANES:]
    return jnp.where(edge_lanes(real.shape, WIDE), real, pltpu.roll(imag, LANES // 2, 1))


def pack_sides(field, at, out):
    packed = folded_edges(field, at)
    lanes = lane_ids(packed.shape)
    for c, gap in enumerate((DOWN, DOWN + LANES // 2)):
        centre = field[at, c, :, :LANES]
        near, far = pltpu.roll(centre, gap, 1), pltpu.roll(centre, gap + 2 * REACH, 1)
        packed = jnp.where((lanes >= gap) & (lanes < gap + REACH), near, packed)
        packed = jnp.where((lanes >= gap + REACH) & (lanes < gap + 2 * REACH), far, packed)
    out[...] = packed


def unpack_sides(centre, sides, out):
    packed = sides[...]
    lanes = lane_ids(packed.shape)
    keep = edge_lanes(packed.shape, DOWN)
    for c, gap in enumerate((DOWN, DOWN + LANES // 2)):
        near = pltpu.roll(packed, LANES - gap, 1)
        far = pltpu.roll(packed, LANES - gap - 2 * REACH, 1)
        out[c, :, :LANES] = jnp.where(
            lanes < REACH, near, jnp.where(lanes >= LANES - REACH, far, centre[c])
        )
        edges = pltpu.roll(packed, LANES // 2, 1) if c else packed
        out[c, :, LANES:] = jnp.where(keep, edges, 0.0)


def pack_carry(field, at, out):
    rows = field.shape[2]
    out[:rows] = field[at, 0, :, :LANES]
    out[rows : 2 * rows] = field[at, 1, :, :LANES]
    edges = folded_edges(field, at)
    part = rows // 4
    packed = edges[:part]
    for b in range(1, 4):
        turned = pltpu.roll(edges[b * part : (b + 1) * part], 16 * b, 1)
        packed = jnp.where(slot_lanes(packed.shape, b), turned, packed)
    out[2 * rows :] = packed


def unpack_carry(packed, out):
    rows = out.shape[1]
    quarter = packed[2 * rows :]
    edges = jnp.concatenate(
        [pltpu.roll(quarter, LANES - 16 * b, 1) if b else quarter for b in range(4)], axis=0
    )
    keep = edge_lanes(edges.shape, 8)
    for c in range(2):
        out[c, :, :LANES] = packed[c * rows : (c + 1) * rows]
        out[c, :, LANES:] = jnp.where(keep, pltpu.roll(edges, LANES // 2, 1) if c else edges, 0.0)


def times(a, b, q_real, q_imag, sign):
    if sign > 0:
        return a * q_real - b * q_imag, a * q_imag + b * q_real
    return a * q_real + b * q_imag, b * q_real - a * q_imag


def sweep(drive, inverse, out, carry, work, planes, rows, reverse):
    rhs, ping, pong = work
    sign = -1 if reverse else 1
    width = out.shape[-1]
    zeros = jnp.zeros((8, width), F32)
    for buffer in (ping, pong):
        for c in range(2):
            buffer[c, :8, :] = zeros
            buffer[c, rows + 8 : rows + 16, :] = zeros

    def beside(buffer, c, r):
        here = buffer[c, r + 8 : r + 16, :]
        return (
            buffer[c, r + 7 : r + 15, :]
            + buffer[c, r + 9 : r + 17, :]
            + (pltpu.roll(here, 1, 1) + pltpu.roll(here, width - 1, 1))
        )

    def plane(step, _):
        z = planes - 1 - step if reverse else step
        for r in range(0, rows, 8):
            strip = slice(r, r + 8)
            a = drive[z, 0, strip, :] + 2.5 * carry[0, strip, :]
            b = drive[z, 1, strip, :] + 2.5 * carry[1, strip, :]
            rhs[0, strip, :] = a
            rhs[1, strip, :] = b
            a, b = times(a, b, inverse[z, 0, strip, :], inverse[z, 1, strip, :], sign)
            ping[0, r + 8 : r + 16, :] = a
            ping[1, r + 8 : r + 16, :] = b
        for r in range(0, rows, 8):
            strip = slice(r, r + 8)
            a = rhs[0, strip, :] + beside(ping, 0, r)
            b = rhs[1, strip, :] + beside(ping, 1, r)
            a, b = times(a, b, inverse[z, 0, strip, :], inverse[z, 1, strip, :], sign)
            pong[0, r + 8 : r + 16, :] = a
            pong[1, r + 8 : r + 16, :] = b
        for r in range(0, rows, 8):
            strip = slice(r, r + 8)
            a = rhs[0, strip, :] + beside(pong, 0, r)
            b = rhs[1, strip, :] + beside(pong, 1, r)
            a, b = times(a, b, inverse[z, 0, strip, :], inverse[z, 1, strip, :], sign)
            out[z, 0, strip, :] = a
            out[z, 1, strip, :] = b
            carry[0, strip, :] = a
            carry[1, strip, :] = b
        return 0

    lax.fori_loop(0, planes, plane, 0)


def sweep_scratch(rows, wide=2 * LANES):
    return [
        VMEM((2, rows, wide), F32),
        VMEM((2, rows, wide), F32),
        VMEM((2, rows + 16, wide), F32),
        VMEM((2, rows + 16, wide), F32),
    ]


def inverses(wavenumber, damping):
    real_diag = 6.0 - wavenumber
    denom = real_diag * real_diag + damping * damping
    return jnp.stack([real_diag / denom, -(damping / denom)], axis=1)


def second_edges_kernel(meta, *refs):
    pack_edges(meta, refs[:MEMBERS], WIDE, False, refs[MEMBERS])


def merge_kernel(meta, *refs):
    pieces, (_, merged, out) = refs[:MEMBERS], refs[MEMBERS:]
    pack_edges(meta, pieces, WIDE, True, out)
    merge_members(meta, pieces, merged)


def observed_edges_kernel(meta, observed, first, second):
    even = meta[1] == 0
    planes, _, shots, rows, count = observed.shape
    lanes = lane_ids((rows, count))
    per_tile = count // NARROW
    sides = {}
    for s in range(shots):
        for p in range(planes):
            for c in range(2):
                tile, j = divmod((s * planes + p) * 2 + c, per_tile)
                at = j * NARROW
                block = observed[p, c, s]
                for side, turn in (("left", at), ("right", (at + NARROW) % count)):
                    got = pltpu.roll(block, turn, 1) if turn else block
                    if j:
                        got = jnp.where(lanes >= at, got, sides[side])
                    sides[side] = got
                if j == per_tile - 1:
                    first[tile] = jnp.where(even, sides["right"], sides["left"])
                    second[tile] = jnp.where(even, sides["left"], sides["right"])


def observed_sends_kernel(meta, observed, first, second, *sends):
    even = meta[1] == 0
    planes, _, _, rows, count = observed.shape
    lanes = lane_ids((rows, count))
    for k, send in enumerate(sends):
        shot = meta[0] ^ k
        for p in range(planes):
            for c in range(2):
                send[2 * p + c] = observed[p, c, shot]
        one, two = first[shot // 2], second[shot // 2]
        right, left = jnp.where(even, one, two), jnp.where(even, two, one)
        odd = lax.rem(shot, 2)
        right = pltpu.roll(right, odd * (count // 2), 1)
        left = pltpu.roll(left, (1 - odd) * (count // 2), 1)
        send[2 * planes] = jnp.where(lanes < count // 2, right, left)


def merge_observed_kernel(meta, *refs):
    pieces, out = refs[:MEMBERS], refs[MEMBERS]
    planes = out.shape[0] // 2
    _, rows, count = pieces[0].shape
    for k, piece in enumerate(pieces):
        who = meta[0] ^ k
        at_plane = (who // 2) * planes
        strip = pl.ds(pl.multiple_of((who % 2) * rows, rows), rows)
        edges = piece[2 * planes]
        for p in range(planes):
            for c in range(2):
                at = (2 * p + c) * NARROW
                out[at_plane + p, c, strip, :LANES] = piece[2 * p + c]
                out[at_plane + p, c, strip, LANES:] = beside_tile(
                    edges,
                    (count - at) % count,
                    edges,
                    (count // 2 - NARROW - at) % count,
                    NARROW,
                )


def centre_kernel(meta, merged, send, field, carry, *work):
    planes, rows = merged.shape[1], merged.shape[3]

    @pl.when(meta[2] == 0)
    def _():
        carry[...] = jnp.zeros_like(carry)
        sweep(merged.at[0], merged.at[1], field, carry, work, planes, rows, False)
        send[...] = carry[...]


def forward_kernel(meta, merged, second, first, drive, inverse, field, send, carry, *work):
    planes, rows = merged.shape[1], merged.shape[3]
    alone = meta[3] == 1
    for f, out in enumerate((drive, inverse)):
        for p in range(planes):
            for c in range(2):
                two = second[f, c]
                two = jnp.where(alone, 0.0, two) if f else two
                out[p, c, :, :LANES] = merged[f, p, c]
                out[p, c, :, LANES:] = unpack_edges(meta, first[f, c], two, p, WIDE)

    @pl.when(meta[2] == 0)
    def _():
        carry[...] = jnp.zeros_like(carry)
        sweep(drive, inverse, field, carry, work, planes, rows, False)
        pack_sides(field, planes - 1, send)


def cut_kernel(height, meta, field, _, *pieces):
    planes, rows = field.shape[0], field.shape[2]
    margin = (rows - 2 * height) // 2
    for k, piece in enumerate(pieces):
        who = meta[0] ^ k
        at_plane = (who // 2) * (planes // 2)
        at_row = pl.multiple_of((who % 2) * height + margin, 8)
        for p in range(planes // 2):
            for c in range(2):
                piece[p, c] = field[at_plane + p, c, pl.ds(at_row, height), :LANES]


def turn_kernel(
    meta,
    drive,
    inverse,
    centre,
    sides,
    observed,
    upper_field,
    field,
    residual,
    adjoint,
    send,
    carry,
    *work,
):
    planes, rows = drive.shape[0], drive.shape[2]
    lower = meta[2] == 1

    @pl.when(jnp.logical_not(lower))
    def _():
        field[...] = upper_field[...]

    @pl.when(lower)
    def _():
        unpack_sides(centre, sides, carry)
        sweep(drive, inverse, field, carry, work, planes, rows, False)

    residual[...] = field[...] - observed[...]

    @pl.when(lower)
    def _():
        carry[...] = jnp.zeros_like(carry)
        sweep(residual, inverse, adjoint, carry, work, planes, rows, True)
        pack_carry(adjoint, 0, send)


def adjoint_kernel(height, meta, residual, inverse, got, field, lower_adjoint, *rest):
    pieces, (adjoint, carry, *work) = rest[:MEMBERS], rest[MEMBERS:]
    planes, rows = residual.shape[0], residual.shape[2]
    margin = (rows - 2 * height) // 2
    upper = meta[2] == 0

    def products(adjoint):
        for k, piece in enumerate(pieces):
            who = meta[0] ^ k
            at_plane = (who // 2) * (planes // 2)
            at_row = pl.multiple_of((who % 2) * height + margin, 8)
            for p in range(planes // 2):
                total = 0.0
                for c in range(2):
                    total += (
                        field[at_plane + p, c, pl.ds(at_row, height), :LANES]
                        * adjoint[at_plane + p, c, pl.ds(at_row, height), :LANES]
                    )
                piece[p] = total * (1.0 / MEMBERS)

    @pl.when(upper)
    def _():
        unpack_carry(got, carry)
        sweep(residual, inverse, adjoint, carry, work, planes, rows, True)
        products(adjoint)

    @pl.when(jnp.logical_not(upper))
    def _():
        products(lower_adjoint)


def field_kernel(meta, *refs):
    out = refs[MEMBERS]
    for k, piece in enumerate(refs[:MEMBERS]):
        out[:, :, meta[0] ^ k] = piece[...]


def body(source, observed, wavenumber, damping):
    own_planes, _, shots, height, width = source.shape
    zi, xi, yi = (lax.axis_index(a) for a in ("depth", "gx", "gy"))
    outermost = (yi == 0) | (yi == lax.axis_size("gy") - 1)
    meta = jnp.stack([2 * (zi % 2) + xi % 2, yi % 2, zi // 2, outermost]).astype(jnp.int32)
    planes, high = 2 * own_planes, 2 * height
    one_group = lax.axis_size("gx") == 2
    rows = high if one_group else high + 2 * WIDE
    tile = (own_planes, 2, height, width)

    inverse = inverses(wavenumber, damping)
    sends = [
        jnp.stack([lax.dynamic_index_in_dim(source, meta[0] ^ k, 2, keepdims=False), inverse])
        for k in range(MEMBERS)
    ]
    observed, *sends = lax.optimization_barrier([observed, *sends])
    pieces = gathered(sends)
    seen_edges = call(observed_edges_kernel, [(2, height, width)] * 2, meta, observed)
    seen_edges = neighbour_swaps(*seen_edges, "gy", 1, ring=True)
    first_seen, *seen_sends = call(
        observed_sends_kernel,
        [(2 * own_planes + 1, height, width)] * MEMBERS,
        meta,
        observed,
        *seen_edges,
    )
    *pieces, first_seen = lax.optimization_barrier([*pieces, first_seen])
    seen_sends = [first_seen, *seen_sends]
    edge_shape = (2, 2, high, width)
    (second,) = call(second_edges_kernel, [edge_shape], meta, *pieces)
    merged, first = call(
        merge_kernel, [(2, planes, 2, high, width), edge_shape], meta, *pieces, second
    )
    if not one_group:
        merged, first, second = (with_row_halo(a, WIDE) for a in (merged, first, second))
    first, second = neighbour_swaps(first, second, "gy", 1, ring=True)
    seen = gathered(seen_sends)

    (centre,) = call(
        centre_kernel,
        [(2, rows, width)],
        meta,
        merged,
        scratch=[VMEM((planes, 2, rows, width), F32), *sweep_scratch(rows, width)],
    )
    centre = depth_pair_swap(centre)

    whole = (planes, 2, rows, 2 * width)
    scratch = sweep_scratch(rows)
    drive, inverse, field, send = call(
        forward_kernel,
        [whole, whole, whole, (rows, width)],
        meta,
        merged,
        second,
        first,
        scratch=scratch,
        cost=30_000_000,
    )
    got = depth_pair_swap(send)
    (seen,) = call(
        merge_observed_kernel, [(planes, 2, high, 2 * width)], meta, *seen, cost=100_000_000
    )
    seen = seen if one_group else with_row_halo(seen, WIDE)
    field, residual, adjoint, send = call(
        turn_kernel,
        [whole, whole, whole, (2 * rows + rows // 4, width)],
        meta,
        drive,
        inverse,
        centre,
        got,
        seen,
        field,
        scratch=scratch,
    )
    got = depth_pair_swap(send)
    pieces = gathered(
        call(lambda *refs: cut_kernel(height, *refs), [tile] * MEMBERS, meta, field, send)
    )
    sums = call(
        lambda *refs: adjoint_kernel(height, *refs),
        [(own_planes, height, width)] * MEMBERS,
        meta,
        residual,
        inverse,
        got,
        field,
        adjoint,
        scratch=[VMEM(whole, F32), *scratch],
    )
    sums = gathered(sums)
    gradient = (sums[0] + sums[1]) + (sums[2] + sums[3])
    (forward_field,) = call(field_kernel, [source.shape], meta, *pieces)
    return forward_field, gradient


def solution(mesh):
    lateral = P("depth", None, None, "gx", "gy")
    return jax.shard_map(
        body,
        mesh=mesh,
        in_specs=(lateral, lateral, P("depth", "gx", "gy"), P("depth", "gx", "gy")),
        out_specs=(lateral, P("depth", "gx", "gy")),
        check_vma=False,
    )
```

```python
import jax
import jax.numpy as jnp
from jax import lax
from jax.experimental import pallas as pl
from jax.experimental.pallas import tpu as pltpu
from jax.sharding import PartitionSpec as P

MEMBERS = 4
WIDE = 32
NARROW = 16
LANES = 128
REACH = 8
DOWN = 24

VMEM = pltpu.VMEM
F32 = jnp.float32


def lane_ids(shape):
    return lax.broadcasted_iota(jnp.int32, shape, len(shape) - 1)


def position():
    zi, xi, yi = (lax.axis_index(a) for a in ("depth", "gx", "gy"))
    outermost = (yi == 0) | (yi == lax.axis_size("gy") - 1)
    return 2 * (zi % 2) + xi % 2, yi % 2, zi // 2, outermost


def call(kernel, outs, *operands, scratch=(), cost=3_000_000):
    return pl.pallas_call(
        lambda *refs: kernel(position(), *refs),
        out_shape=[jax.ShapeDtypeStruct(shape, F32) for shape in outs],
        in_specs=[pl.BlockSpec(memory_space=VMEM)] * len(operands),
        out_specs=[pl.BlockSpec(memory_space=VMEM)] * len(outs),
        scratch_shapes=list(scratch),
        cost_estimate=pl.CostEstimate(flops=0, bytes_accessed=cost, transcendentals=0),
        compiler_params=pltpu.CompilerParams(vmem_limit_bytes=8 * 1024 * 1024),
    )(*operands)


def member_swap(block, offset):
    nz, nx = lax.axis_size("depth"), lax.axis_size("gx")
    dz, dx = offset >> 1, offset & 1
    pairs = [(z * nx + x, (z ^ dz) * nx + (x ^ dx)) for z in range(nz) for x in range(nx)]
    return lax.ppermute(block, ("depth", "gx"), pairs)


def gathered(sends):
    return [sends[0]] + [member_swap(sends[k], k) for k in range(1, MEMBERS)]


def depth_pair_swap(block):
    return lax.ppermute(block, "depth", [(z, z ^ 2) for z in range(lax.axis_size("depth"))])


def neighbour_swaps(first, second, axis, stride, ring=False):
    size = lax.axis_size(axis)
    count = size // stride

    def pairs(start):
        found = []
        for low in range(start, count - 1, 2):
            for part in range(stride):
                a, b = low * stride + part, (low + 1) * stride + part
                found += [(a, b), (b, a)]
        return found

    ends = [(i, size - stride + i) for i in range(stride)] if ring and count % 2 == 0 else []
    ends += [(b, a) for a, b in ends]
    got_second = lax.ppermute(second, axis, pairs(1) + ends) if count > 2 else jnp.zeros_like(second)
    got_first = lax.ppermute(first, axis, pairs(0)) if count > 1 else jnp.zeros_like(first)
    return got_first, got_second


def with_row_halo(block, width):
    groups = lax.axis_size("gx") // 2
    if groups == 1:
        return block
    even = (lax.axis_index("gx") // 2) % 2 == 0
    top, bottom = block[..., :width, :], block[..., -width:, :]
    one, two = neighbour_swaps(
        jnp.where(even, bottom, top), jnp.where(even, top, bottom), "gx", 2
    )
    above, below = jnp.where(even, two, one), jnp.where(even, one, two)
    return jnp.concatenate([above, block, below], axis=-2)


def merge_members(meta, pieces, out):
    me = meta[0]
    for k, piece in enumerate(pieces):
        fields, planes, _, rows, _ = piece.shape
        who = me ^ k
        at_plane = (who // 2) * planes
        at_row = pl.multiple_of((who % 2) * rows, rows)
        for f in range(fields):
            for p in range(planes):
                for c in range(2):
                    out[f, at_plane + p, c, pl.ds(at_row, rows), :] = piece[f, p, c]


def pack_edges(meta, pieces, width, first, out):
    me, even = meta[0], meta[1] == 0
    fields, planes, _, rows, count = pieces[0].shape
    lanes = lane_ids((rows, count))

    def pack(lower, right):
        for k in range(2):
            strip = pl.ds(pl.multiple_of(((me ^ k) % 2) * rows, rows), rows)
            pair = (pieces[k + 2], pieces[k]) if lower else (pieces[k], pieces[k + 2])
            for f in range(fields):
                for c in range(2):
                    side = None
                    for j in range(2 * planes):
                        got = pair[j // planes][f, j % planes, c]
                        turn = (j * width + (width if right else 0)) % count
                        got = pltpu.roll(got, turn, 1) if turn else got
                        side = got if j == 0 else jnp.where(lanes >= j * width, got, side)
                    out[f, c, strip, :] = side

    for lower in (False, True):
        for right in (False, True):
            pl.when(((me >= 2) == lower) & ((even == first) == right))(
                lambda lower=lower, right=right: pack(lower, right)
            )


def beside_tile(right, right_turn, left, left_turn, width):
    lanes = lane_ids(right.shape)
    right = pltpu.roll(right, right_turn, 1) if right_turn else right
    left = pltpu.roll(left, left_turn, 1) if left_turn else left
    return jnp.where(lanes < width, right, jnp.where(lanes >= LANES - width, left, 0.0))


def edge_lanes(shape, margin):
    lanes = lane_ids(shape)
    return (lanes < margin) | (lanes >= LANES - margin)


def slot_lanes(shape, block):
    return lax.rem(lane_ids(shape) + (LANES - 16 * block - LANES // 2 + 8), LANES // 2) < 16


def folded_edges(field, at):
    real, imag = field[at, 0, :, LANES:], field[at, 1, :, LANES:]
    return jnp.where(edge_lanes(real.shape, WIDE), real, pltpu.roll(imag, LANES // 2, 1))


def pack_sides(field, at, out):
    packed = folded_edges(field, at)
    lanes = lane_ids(packed.shape)
    for c, gap in enumerate((DOWN, DOWN + LANES // 2)):
        centre = field[at, c, :, :LANES]
        near, far = pltpu.roll(centre, gap, 1), pltpu.roll(centre, gap + 2 * REACH, 1)
        packed = jnp.where((lanes >= gap) & (lanes < gap + REACH), near, packed)
        packed = jnp.where((lanes >= gap + REACH) & (lanes < gap + 2 * REACH), far, packed)
    out[...] = packed


def unpack_sides(centre, sides, out):
    packed = sides[...]
    lanes = lane_ids(packed.shape)
    keep = edge_lanes(packed.shape, DOWN)
    for c, gap in enumerate((DOWN, DOWN + LANES // 2)):
        near = pltpu.roll(packed, LANES - gap, 1)
        far = pltpu.roll(packed, LANES - gap - 2 * REACH, 1)
        out[c, :, :LANES] = jnp.where(
            lanes < REACH, near, jnp.where(lanes >= LANES - REACH, far, centre[c])
        )
        edges = pltpu.roll(packed, LANES // 2, 1) if c else packed
        out[c, :, LANES:] = jnp.where(keep, edges, 0.0)


def pack_carry(field, at, out):
    rows = field.shape[2]
    out[:rows] = field[at, 0, :, :LANES]
    out[rows : 2 * rows] = field[at, 1, :, :LANES]
    edges = folded_edges(field, at)
    part = rows // 4
    packed = edges[:part]
    for b in range(1, 4):
        turned = pltpu.roll(edges[b * part : (b + 1) * part], 16 * b, 1)
        packed = jnp.where(slot_lanes(packed.shape, b), turned, packed)
    out[2 * rows :] = packed


def unpack_carry(packed, out):
    rows = out.shape[1]
    quarter = packed[2 * rows :]
    edges = jnp.concatenate(
        [pltpu.roll(quarter, LANES - 16 * b, 1) if b else quarter for b in range(4)], axis=0
    )
    keep = edge_lanes(edges.shape, 8)
    for c in range(2):
        out[c, :, :LANES] = packed[c * rows : (c + 1) * rows]
        out[c, :, LANES:] = jnp.where(keep, pltpu.roll(edges, LANES // 2, 1) if c else edges, 0.0)


def times(a, b, q_real, q_imag, sign):
    if sign > 0:
        return a * q_real - b * q_imag, a * q_imag + b * q_real
    return a * q_real + b * q_imag, b * q_real - a * q_imag


def beside_each_other(refs):
    def read(z, c, strip):
        parts = [ref[z, c, strip, :] for ref in refs]
        return parts[0] if len(parts) == 1 else jnp.concatenate(parts, axis=1)

    return read


def sweep(drive, inverse, out, carry, work, planes, rows, reverse):
    drive, inverse = beside_each_other(drive), beside_each_other(inverse)
    rhs, ping, pong = work
    sign = -1 if reverse else 1
    width = out.shape[-1]
    zeros = jnp.zeros((8, width), F32)
    for buffer in (ping, pong):
        for c in range(2):
            buffer[c, :8, :] = zeros
            buffer[c, rows + 8 : rows + 16, :] = zeros

    def beside(buffer, c, r):
        here = buffer[c, r + 8 : r + 16, :]
        return (
            buffer[c, r + 7 : r + 15, :]
            + buffer[c, r + 9 : r + 17, :]
            + (pltpu.roll(here, 1, 1) + pltpu.roll(here, width - 1, 1))
        )

    def plane(step, _):
        z = planes - 1 - step if reverse else step
        for r in range(0, rows, 8):
            strip = slice(r, r + 8)
            a = drive(z, 0, strip) + 2.5 * carry[0, strip, :]
            b = drive(z, 1, strip) + 2.5 * carry[1, strip, :]
            rhs[0, strip, :] = a
            rhs[1, strip, :] = b
            a, b = times(a, b, inverse(z, 0, strip), inverse(z, 1, strip), sign)
            ping[0, r + 8 : r + 16, :] = a
            ping[1, r + 8 : r + 16, :] = b
        for r in range(0, rows, 8):
            strip = slice(r, r + 8)
            a = rhs[0, strip, :] + beside(ping, 0, r)
            b = rhs[1, strip, :] + beside(ping, 1, r)
            a, b = times(a, b, inverse(z, 0, strip), inverse(z, 1, strip), sign)
            pong[0, r + 8 : r + 16, :] = a
            pong[1, r + 8 : r + 16, :] = b
        for r in range(0, rows, 8):
            strip = slice(r, r + 8)
            a = rhs[0, strip, :] + beside(pong, 0, r)
            b = rhs[1, strip, :] + beside(pong, 1, r)
            a, b = times(a, b, inverse(z, 0, strip), inverse(z, 1, strip), sign)
            out[z, 0, strip, :] = a
            out[z, 1, strip, :] = b
            carry[0, strip, :] = a
            carry[1, strip, :] = b
        return 0

    lax.fori_loop(0, planes, plane, 0)


def sweep_scratch(rows, wide=2 * LANES):
    return [
        VMEM((2, rows, wide), F32),
        VMEM((2, rows, wide), F32),
        VMEM((2, rows + 16, wide), F32),
        VMEM((2, rows + 16, wide), F32),
    ]


def inverses(wavenumber, damping):
    real_diag = 6.0 - wavenumber
    denom = real_diag * real_diag + damping * damping
    return jnp.stack([real_diag / denom, -(damping / denom)], axis=1)


def second_edges_kernel(meta, *refs):
    pack_edges(meta, refs[:MEMBERS], WIDE, False, refs[MEMBERS])


def merge_kernel(meta, *refs):
    pieces, (_, merged, out) = refs[:MEMBERS], refs[MEMBERS:]
    pack_edges(meta, pieces, WIDE, True, out)
    merge_members(meta, pieces, merged)


def observed_edges_kernel(meta, observed, first, second):
    even = meta[1] == 0
    planes, _, shots, rows, count = observed.shape
    lanes = lane_ids((rows, count))
    per_tile = count // NARROW
    sides = {}
    for s in range(shots):
        for p in range(planes):
            for c in range(2):
                tile, j = divmod((s * planes + p) * 2 + c, per_tile)
                at = j * NARROW
                block = observed[p, c, s]
                for side, turn in (("left", at), ("right", (at + NARROW) % count)):
                    got = pltpu.roll(block, turn, 1) if turn else block
                    if j:
                        got = jnp.where(lanes >= at, got, sides[side])
                    sides[side] = got
                if j == per_tile - 1:
                    first[tile] = jnp.where(even, sides["right"], sides["left"])
                    second[tile] = jnp.where(even, sides["left"], sides["right"])


def observed_sends_kernel(meta, observed, first, second, *sends):
    even = meta[1] == 0
    planes, _, _, rows, count = observed.shape
    lanes = lane_ids((rows, count))
    for k, send in enumerate(sends):
        shot = meta[0] ^ k
        for p in range(planes):
            for c in range(2):
                send[2 * p + c] = observed[p, c, shot]
        one, two = first[shot // 2], second[shot // 2]
        right, left = jnp.where(even, one, two), jnp.where(even, two, one)
        odd = lax.rem(shot, 2)
        right = pltpu.roll(right, odd * (count // 2), 1)
        left = pltpu.roll(left, (1 - odd) * (count // 2), 1)
        send[2 * planes] = jnp.where(lanes < count // 2, right, left)


def merge_observed_kernel(meta, *refs):
    pieces, out = refs[:MEMBERS], refs[MEMBERS]
    planes = out.shape[0] // 2
    _, rows, count = pieces[0].shape
    for k, piece in enumerate(pieces):
        who = meta[0] ^ k
        at_plane = (who // 2) * planes
        strip = pl.ds(pl.multiple_of((who % 2) * rows, rows), rows)
        edges = piece[2 * planes]
        for p in range(planes):
            for c in range(2):
                at = (2 * p + c) * NARROW
                out[at_plane + p, c, strip, :LANES] = piece[2 * p + c]
                out[at_plane + p, c, strip, LANES:] = beside_tile(
                    edges,
                    (count - at) % count,
                    edges,
                    (count // 2 - NARROW - at) % count,
                    NARROW,
                )


def centre_kernel(meta, merged, send, field, carry, *work):
    planes, rows = merged.shape[1], merged.shape[3]

    @pl.when(meta[2] == 0)
    def _():
        carry[...] = jnp.zeros_like(carry)
        sweep([merged.at[0]], [merged.at[1]], field, carry, work, planes, rows, False)
        send[...] = carry[...]


def forward_kernel(meta, merged, second, first, sides, field, send, carry, *work):
    planes, rows = merged.shape[1], merged.shape[3]
    even, alone = meta[1] == 0, meta[3]
    for f in range(2):
        for c in range(2):
            for r in range(0, rows, 32):
                strip = slice(r, r + 32)
                one, two = first[f, c, strip, :], second[f, c, strip, :]
                two = jnp.where(alone, 0.0, two) if f else two
                right, left = jnp.where(even, one, two), jnp.where(even, two, one)
                for p in range(planes):
                    at = p * WIDE
                    sides[f, p, c, strip, :] = beside_tile(
                        right, (LANES - at) % LANES, left, (2 * LANES - WIDE - at) % LANES, WIDE
                    )

    @pl.when(meta[2] == 0)
    def _():
        carry[...] = jnp.zeros_like(carry)
        drive, inverse = ([merged.at[f], sides.at[f]] for f in range(2))
        sweep(drive, inverse, field, carry, work, planes, rows, False)
        pack_sides(field, planes - 1, send)


def cut_kernel(height, meta, field, _, *pieces):
    planes, rows = field.shape[0], field.shape[2]
    margin = (rows - 2 * height) // 2
    for k, piece in enumerate(pieces):
        who = meta[0] ^ k
        at_plane = (who // 2) * (planes // 2)
        at_row = pl.multiple_of((who % 2) * height + margin, 8)
        for p in range(planes // 2):
            for c in range(2):
                piece[p, c] = field[at_plane + p, c, pl.ds(at_row, height), :LANES]


def turn_kernel(
    meta,
    merged,
    beside,
    centre,
    sides,
    observed,
    upper_field,
    field,
    residual,
    adjoint,
    send,
    carry,
    *work,
):
    planes, rows = merged.shape[1], merged.shape[3]
    drive, inverse = ([merged.at[f], beside.at[f]] for f in range(2))
    lower = meta[2] == 1

    @pl.when(jnp.logical_not(lower))
    def _():
        field[...] = upper_field[...]

    @pl.when(lower)
    def _():
        unpack_sides(centre, sides, carry)
        sweep(drive, inverse, field, carry, work, planes, rows, False)

    residual[...] = field[...] - observed[...]

    @pl.when(lower)
    def _():
        carry[...] = jnp.zeros_like(carry)
        sweep([residual], inverse, adjoint, carry, work, planes, rows, True)
        pack_carry(adjoint, 0, send)


def adjoint_kernel(height, meta, residual, merged, beside, got, field, lower_adjoint, *rest):
    pieces, (adjoint, carry, *work) = rest[:MEMBERS], rest[MEMBERS:]
    planes, rows = residual.shape[0], residual.shape[2]
    margin = (rows - 2 * height) // 2
    upper = meta[2] == 0
    inverse = [merged.at[1], beside.at[1]]

    def products(adjoint):
        for k, piece in enumerate(pieces):
            who = meta[0] ^ k
            at_plane = (who // 2) * (planes // 2)
            at_row = pl.multiple_of((who % 2) * height + margin, 8)
            for p in range(planes // 2):
                total = 0.0
                for c in range(2):
                    total += (
                        field[at_plane + p, c, pl.ds(at_row, height), :LANES]
                        * adjoint[at_plane + p, c, pl.ds(at_row, height), :LANES]
                    )
                piece[p] = total * (1.0 / MEMBERS)

    @pl.when(upper)
    def _():
        unpack_carry(got, carry)
        sweep([residual], inverse, adjoint, carry, work, planes, rows, True)
        products(adjoint)

    @pl.when(jnp.logical_not(upper))
    def _():
        products(lower_adjoint)


def field_kernel(meta, *refs):
    out = refs[MEMBERS]
    for k, piece in enumerate(refs[:MEMBERS]):
        out[:, :, meta[0] ^ k] = piece[...]


def body(source, observed, wavenumber, damping):
    own_planes, _, shots, height, width = source.shape
    member = position()[0]
    planes, high = 2 * own_planes, 2 * height
    one_group = lax.axis_size("gx") == 2
    rows = high if one_group else high + 2 * WIDE
    tile = (own_planes, 2, height, width)

    inverse = inverses(wavenumber, damping)
    sends = [
        jnp.stack([lax.dynamic_index_in_dim(source, member ^ k, 2, keepdims=False), inverse])
        for k in range(MEMBERS)
    ]
    observed, *sends = lax.optimization_barrier([observed, *sends])
    pieces = gathered(sends)
    seen_edges = call(observed_edges_kernel, [(2, height, width)] * 2, observed)
    seen_edges = neighbour_swaps(*seen_edges, "gy", 1, ring=True)
    first_seen, *seen_sends = call(
        observed_sends_kernel,
        [(2 * own_planes + 1, height, width)] * MEMBERS,
        observed,
        *seen_edges,
    )
    *pieces, first_seen = lax.optimization_barrier([*pieces, first_seen])
    seen_sends = [first_seen, *seen_sends]
    edge_shape = (2, 2, high, width)
    (second,) = call(second_edges_kernel, [edge_shape], *pieces)
    merged, first = call(
        merge_kernel, [(2, planes, 2, high, width), edge_shape], *pieces, second
    )
    if not one_group:
        merged, first, second = (with_row_halo(a, WIDE) for a in (merged, first, second))
    first, second = neighbour_swaps(first, second, "gy", 1, ring=True)
    seen = gathered(seen_sends)

    (centre,) = call(
        centre_kernel,
        [(2, rows, width)],
        merged,
        scratch=[VMEM((planes, 2, rows, width), F32), *sweep_scratch(rows, width)],
    )
    centre = depth_pair_swap(centre)

    whole = (planes, 2, rows, 2 * width)
    scratch = sweep_scratch(rows)
    beside, field, send = call(
        forward_kernel,
        [(2, planes, 2, rows, width), whole, (rows, width)],
        merged,
        second,
        first,
        scratch=scratch,
        cost=30_000_000,
    )
    got = depth_pair_swap(send)
    (seen,) = call(
        merge_observed_kernel, [(planes, 2, high, 2 * width)], *seen, cost=100_000_000
    )
    seen = seen if one_group else with_row_halo(seen, WIDE)
    field, residual, adjoint, send = call(
        turn_kernel,
        [whole, whole, whole, (2 * rows + rows // 4, width)],
        merged,
        beside,
        centre,
        got,
        seen,
        field,
        scratch=scratch,
    )
    got = depth_pair_swap(send)
    pieces = gathered(
        call(lambda *refs: cut_kernel(height, *refs), [tile] * MEMBERS, field, send)
    )
    sums = call(
        lambda *refs: adjoint_kernel(height, *refs),
        [(own_planes, height, width)] * MEMBERS,
        residual,
        merged,
        beside,
        got,
        field,
        adjoint,
        scratch=[VMEM(whole, F32), *scratch],
    )
    sums = gathered(sums)
    gradient = (sums[0] + sums[1]) + (sums[2] + sums[3])
    (forward_field,) = call(field_kernel, [source.shape], *pieces)
    return forward_field, gradient


def solution(mesh):
    lateral = P("depth", None, None, "gx", "gy")
    return jax.shard_map(
        body,
        mesh=mesh,
        in_specs=(lateral, lateral, P("depth", "gx", "gy"), P("depth", "gx", "gy")),
        out_specs=(lateral, P("depth", "gx", "gy")),
        check_vma=False,
    )
```

```python
import jax
import jax.numpy as jnp
from jax import lax
from jax.experimental import pallas as pl
from jax.experimental.pallas import tpu as pltpu
from jax.sharding import PartitionSpec as P

MEMBERS = 4
WIDE = 32
NARROW = 16
LANES = 128
ALONG, ACROSS = (0, 1), (2, 3)
REACH = 8
DOWN = 24

VMEM = pltpu.VMEM
F32 = jnp.float32


def lane_ids(shape):
    return lax.broadcasted_iota(jnp.int32, shape, len(shape) - 1)


def position():
    zi, xi, yi = (lax.axis_index(a) for a in ("depth", "gx", "gy"))
    outermost = (yi == 0) | (yi == lax.axis_size("gy") - 1)
    return 2 * (zi % 2) + xi % 2, yi % 2, zi // 2, outermost


def call(kernel, outs, *operands, scratch=(), cost=3_000_000):
    return pl.pallas_call(
        lambda *refs: kernel(position(), *refs),
        out_shape=[jax.ShapeDtypeStruct(shape, F32) for shape in outs],
        in_specs=[pl.BlockSpec(memory_space=VMEM)] * len(operands),
        out_specs=[pl.BlockSpec(memory_space=VMEM)] * len(outs),
        scratch_shapes=list(scratch),
        cost_estimate=pl.CostEstimate(flops=0, bytes_accessed=cost, transcendentals=0),
        compiler_params=pltpu.CompilerParams(vmem_limit_bytes=8 * 1024 * 1024),
    )(*operands)


def member_swap(block, offset):
    nz, nx = lax.axis_size("depth"), lax.axis_size("gx")
    dz, dx = offset >> 1, offset & 1
    pairs = [(z * nx + x, (z ^ dz) * nx + (x ^ dx)) for z in range(nz) for x in range(nx)]
    return lax.ppermute(block, ("depth", "gx"), pairs)


def gathered(sends):
    return [member_swap(sends[k], k) for k in (3, 2, 1)] + [sends[0]]


def depth_pair_swap(block):
    return lax.ppermute(block, "depth", [(z, z ^ 2) for z in range(lax.axis_size("depth"))])


def neighbour_swaps(first, second, axis, stride, ring=False):
    size = lax.axis_size(axis)
    count = size // stride

    def pairs(start):
        found = []
        for low in range(start, count - 1, 2):
            for part in range(stride):
                a, b = low * stride + part, (low + 1) * stride + part
                found += [(a, b), (b, a)]
        return found

    ends = [(i, size - stride + i) for i in range(stride)] if ring and count % 2 == 0 else []
    ends += [(b, a) for a, b in ends]
    got_second = lax.ppermute(second, axis, pairs(1) + ends) if count > 2 else jnp.zeros_like(second)
    got_first = lax.ppermute(first, axis, pairs(0)) if count > 1 else jnp.zeros_like(first)
    return got_first, got_second


def with_row_halo(block, width):
    groups = lax.axis_size("gx") // 2
    if groups == 1:
        return block
    even = (lax.axis_index("gx") // 2) % 2 == 0
    top, bottom = block[..., :width, :], block[..., -width:, :]
    one, two = neighbour_swaps(
        jnp.where(even, bottom, top), jnp.where(even, top, bottom), "gx", 2
    )
    above, below = jnp.where(even, two, one), jnp.where(even, one, two)
    return jnp.concatenate([above, block, below], axis=-2)


def merge_members(meta, pieces, out):
    me = meta[0]
    for k, piece in enumerate(pieces):
        fields, planes, _, rows, _ = piece.shape
        who = me ^ k
        at_plane = (who // 2) * planes
        at_row = pl.multiple_of((who % 2) * rows, rows)
        for f in range(fields):
            for p in range(planes):
                for c in range(2):
                    out[f, at_plane + p, c, pl.ds(at_row, rows), :] = piece[f, p, c]


def pack_edges(meta, pieces, width, first, out):
    me, even = meta[0], meta[1] == 0
    fields, planes, _, rows, count = pieces[0].shape
    lanes = lane_ids((rows, count))

    def pack(lower, right):
        for k in range(2):
            strip = pl.ds(pl.multiple_of(((me ^ k) % 2) * rows, rows), rows)
            pair = (pieces[k + 2], pieces[k]) if lower else (pieces[k], pieces[k + 2])
            for f in range(fields):
                for c in range(2):
                    side = None
                    for j in range(2 * planes):
                        got = pair[j // planes][f, j % planes, c]
                        turn = (j * width + (width if right else 0)) % count
                        got = pltpu.roll(got, turn, 1) if turn else got
                        side = got if j == 0 else jnp.where(lanes >= j * width, got, side)
                    out[f, c, strip, :] = side

    for lower in (False, True):
        for right in (False, True):
            pl.when(((me >= 2) == lower) & ((even == first) == right))(
                lambda lower=lower, right=right: pack(lower, right)
            )


def beside_tile(right, right_turn, left, left_turn, width):
    lanes = lane_ids(right.shape)
    right = pltpu.roll(right, right_turn, 1) if right_turn else right
    left = pltpu.roll(left, left_turn, 1) if left_turn else left
    return jnp.where(lanes < width, right, jnp.where(lanes >= LANES - width, left, 0.0))


def edge_lanes(shape, margin):
    lanes = lane_ids(shape)
    return (lanes < margin) | (lanes >= LANES - margin)


def slot_lanes(shape, block):
    return lax.rem(lane_ids(shape) + (LANES - 16 * block - LANES // 2 + 8), LANES // 2) < 16


def folded_edges(field, at):
    real, imag = field[at, 0, :, LANES:], field[at, 1, :, LANES:]
    return jnp.where(edge_lanes(real.shape, WIDE), real, pltpu.roll(imag, LANES // 2, 1))


def pack_sides(field, at, out):
    packed = folded_edges(field, at)
    lanes = lane_ids(packed.shape)
    for c, gap in enumerate((DOWN, DOWN + LANES // 2)):
        centre = field[at, c, :, :LANES]
        near, far = pltpu.roll(centre, gap, 1), pltpu.roll(centre, gap + 2 * REACH, 1)
        packed = jnp.where((lanes >= gap) & (lanes < gap + REACH), near, packed)
        packed = jnp.where((lanes >= gap + REACH) & (lanes < gap + 2 * REACH), far, packed)
    out[...] = packed


def unpack_sides(centre, sides, out):
    packed = sides[...]
    lanes = lane_ids(packed.shape)
    keep = edge_lanes(packed.shape, DOWN)
    for c, gap in enumerate((DOWN, DOWN + LANES // 2)):
        near = pltpu.roll(packed, LANES - gap, 1)
        far = pltpu.roll(packed, LANES - gap - 2 * REACH, 1)
        out[c, :, :LANES] = jnp.where(
            lanes < REACH, near, jnp.where(lanes >= LANES - REACH, far, centre[c])
        )
        edges = pltpu.roll(packed, LANES // 2, 1) if c else packed
        out[c, :, LANES:] = jnp.where(keep, edges, 0.0)


def pack_carry(field, at, out):
    rows = field.shape[2]
    out[:rows] = field[at, 0, :, :LANES]
    out[rows : 2 * rows] = field[at, 1, :, :LANES]
    edges = folded_edges(field, at)
    part = rows // 4
    packed = edges[:part]
    for b in range(1, 4):
        turned = pltpu.roll(edges[b * part : (b + 1) * part], 16 * b, 1)
        packed = jnp.where(slot_lanes(packed.shape, b), turned, packed)
    out[2 * rows :] = packed


def unpack_carry(packed, out):
    rows = out.shape[1]
    quarter = packed[2 * rows :]
    edges = jnp.concatenate(
        [pltpu.roll(quarter, LANES - 16 * b, 1) if b else quarter for b in range(4)], axis=0
    )
    keep = edge_lanes(edges.shape, 8)
    for c in range(2):
        out[c, :, :LANES] = packed[c * rows : (c + 1) * rows]
        out[c, :, LANES:] = jnp.where(keep, pltpu.roll(edges, LANES // 2, 1) if c else edges, 0.0)


def times(a, b, q_real, q_imag, sign):
    if sign > 0:
        return a * q_real - b * q_imag, a * q_imag + b * q_real
    return a * q_real + b * q_imag, b * q_real - a * q_imag


def beside_each_other(refs):
    def read(z, c, strip):
        parts = [ref[z, c, strip, :] for ref in refs]
        return parts[0] if len(parts) == 1 else jnp.concatenate(parts, axis=1)

    return read


def sweep(drive, inverse, out, carry, work, planes, rows, reverse):
    drive, inverse = beside_each_other(drive), beside_each_other(inverse)
    rhs, ping, pong = work
    sign = -1 if reverse else 1
    width = out.shape[-1]
    zeros = jnp.zeros((8, width), F32)
    for buffer in (ping, pong):
        for c in range(2):
            buffer[c, :8, :] = zeros
            buffer[c, rows + 8 : rows + 16, :] = zeros

    def beside(buffer, c, r):
        here = buffer[c, r + 8 : r + 16, :]
        return (
            buffer[c, r + 7 : r + 15, :]
            + buffer[c, r + 9 : r + 17, :]
            + (pltpu.roll(here, 1, 1) + pltpu.roll(here, width - 1, 1))
        )

    def plane(step, _):
        z = planes - 1 - step if reverse else step
        for r in range(0, rows, 8):
            strip = slice(r, r + 8)
            a = drive(z, 0, strip) + 2.5 * carry[0, strip, :]
            b = drive(z, 1, strip) + 2.5 * carry[1, strip, :]
            rhs[0, strip, :] = a
            rhs[1, strip, :] = b
            a, b = times(a, b, inverse(z, 0, strip), inverse(z, 1, strip), sign)
            ping[0, r + 8 : r + 16, :] = a
            ping[1, r + 8 : r + 16, :] = b
        for r in range(0, rows, 8):
            strip = slice(r, r + 8)
            a = rhs[0, strip, :] + beside(ping, 0, r)
            b = rhs[1, strip, :] + beside(ping, 1, r)
            a, b = times(a, b, inverse(z, 0, strip), inverse(z, 1, strip), sign)
            pong[0, r + 8 : r + 16, :] = a
            pong[1, r + 8 : r + 16, :] = b
        for r in range(0, rows, 8):
            strip = slice(r, r + 8)
            a = rhs[0, strip, :] + beside(pong, 0, r)
            b = rhs[1, strip, :] + beside(pong, 1, r)
            a, b = times(a, b, inverse(z, 0, strip), inverse(z, 1, strip), sign)
            out[z, 0, strip, :] = a
            out[z, 1, strip, :] = b
            carry[0, strip, :] = a
            carry[1, strip, :] = b
        return 0

    lax.fori_loop(0, planes, plane, 0)


def sweep_scratch(rows, wide=2 * LANES):
    return [
        VMEM((2, rows, wide), F32),
        VMEM((2, rows, wide), F32),
        VMEM((2, rows + 16, wide), F32),
        VMEM((2, rows + 16, wide), F32),
    ]


def inverses(wavenumber, damping):
    real_diag = 6.0 - wavenumber
    denom = real_diag * real_diag + damping * damping
    return jnp.stack([real_diag / denom, -(damping / denom)], axis=1)


def second_edges_kernel(meta, *refs):
    pack_edges(meta, refs[MEMBERS - 1 :: -1], WIDE, False, refs[MEMBERS])


def merge_kernel(meta, *refs):
    pieces, (_, merged, out) = refs[MEMBERS - 1 :: -1], refs[MEMBERS:]
    pack_edges(meta, pieces, WIDE, True, out)
    merge_members(meta, pieces, merged)


def prepare_kernel(ks, meta, source, inverse, *refs):
    for k, send in zip(ks, refs[-len(ks) :]):
        send[0] = source[:, :, meta[0] ^ k]
        send[1] = inverse[...]


def observed_edges_kernel(meta, observed, first, second):
    even = meta[1] == 0
    planes, _, shots, rows, count = observed.shape
    lanes = lane_ids((rows, count))
    per_tile = count // NARROW
    sides = {}
    for s in range(shots):
        for p in range(planes):
            for c in range(2):
                tile, j = divmod((s * planes + p) * 2 + c, per_tile)
                at = j * NARROW
                block = observed[p, c, s]
                for side, turn in (("left", at), ("right", (at + NARROW) % count)):
                    got = pltpu.roll(block, turn, 1) if turn else block
                    if j:
                        got = jnp.where(lanes >= at, got, sides[side])
                    sides[side] = got
                if j == per_tile - 1:
                    first[tile] = jnp.where(even, sides["right"], sides["left"])
                    second[tile] = jnp.where(even, sides["left"], sides["right"])


def observed_sends_kernel(ks, meta, observed, first, second, *refs):
    even = meta[1] == 0
    planes, _, _, rows, count = observed.shape
    lanes = lane_ids((rows, count))
    for k, send in zip(ks, refs[-len(ks) :]):
        shot = meta[0] ^ k
        for p in range(planes):
            for c in range(2):
                send[2 * p + c] = observed[p, c, shot]
        one, two = first[shot // 2], second[shot // 2]
        right, left = jnp.where(even, one, two), jnp.where(even, two, one)
        odd = lax.rem(shot, 2)
        right = pltpu.roll(right, odd * (count // 2), 1)
        left = pltpu.roll(left, (1 - odd) * (count // 2), 1)
        send[2 * planes] = jnp.where(lanes < count // 2, right, left)


def merge_observed_kernel(meta, *refs):
    pieces, out = refs[MEMBERS - 1 :: -1], refs[MEMBERS]
    planes = out.shape[0] // 2
    _, rows, count = pieces[0].shape
    for k, piece in enumerate(pieces):
        who = meta[0] ^ k
        at_plane = (who // 2) * planes
        strip = pl.ds(pl.multiple_of((who % 2) * rows, rows), rows)
        edges = piece[2 * planes]
        for p in range(planes):
            for c in range(2):
                at = (2 * p + c) * NARROW
                out[at_plane + p, c, strip, :LANES] = piece[2 * p + c]
                out[at_plane + p, c, strip, LANES:] = beside_tile(
                    edges,
                    (count - at) % count,
                    edges,
                    (count // 2 - NARROW - at) % count,
                    NARROW,
                )


def centre_kernel(meta, merged, send, field, carry, *work):
    planes, rows = merged.shape[1], merged.shape[3]

    @pl.when(meta[2] == 0)
    def _():
        carry[...] = jnp.zeros_like(carry)
        sweep([merged.at[0]], [merged.at[1]], field, carry, work, planes, rows, False)
        send[...] = carry[...]


def forward_kernel(meta, merged, second, first, sides, field, send, carry, *work):
    planes, rows = merged.shape[1], merged.shape[3]
    even, alone = meta[1] == 0, meta[3]
    for f in range(2):
        for c in range(2):
            for r in range(0, rows, 32):
                strip = slice(r, r + 32)
                one, two = first[f, c, strip, :], second[f, c, strip, :]
                two = jnp.where(alone, 0.0, two) if f else two
                right, left = jnp.where(even, one, two), jnp.where(even, two, one)
                for p in range(planes):
                    at = p * WIDE
                    sides[f, p, c, strip, :] = beside_tile(
                        right, (LANES - at) % LANES, left, (2 * LANES - WIDE - at) % LANES, WIDE
                    )

    @pl.when(meta[2] == 0)
    def _():
        carry[...] = jnp.zeros_like(carry)
        drive, inverse = ([merged.at[f], sides.at[f]] for f in range(2))
        sweep(drive, inverse, field, carry, work, planes, rows, False)
        pack_sides(field, planes - 1, send)


def cut_kernel(height, meta, field, _, *pieces):
    planes, rows = field.shape[0], field.shape[2]
    margin = (rows - 2 * height) // 2
    for k, piece in enumerate(pieces):
        who = meta[0] ^ k
        at_plane = (who // 2) * (planes // 2)
        at_row = pl.multiple_of((who % 2) * height + margin, 8)
        for p in range(planes // 2):
            for c in range(2):
                piece[p, c] = field[at_plane + p, c, pl.ds(at_row, height), :LANES]


def turn_kernel(
    meta,
    merged,
    beside,
    centre,
    sides,
    observed,
    upper_field,
    field,
    residual,
    adjoint,
    send,
    carry,
    *work,
):
    planes, rows = merged.shape[1], merged.shape[3]
    drive, inverse = ([merged.at[f], beside.at[f]] for f in range(2))
    lower = meta[2] == 1

    @pl.when(jnp.logical_not(lower))
    def _():
        field[...] = upper_field[...]

    @pl.when(lower)
    def _():
        unpack_sides(centre, sides, carry)
        sweep(drive, inverse, field, carry, work, planes, rows, False)

    residual[...] = field[...] - observed[...]

    @pl.when(lower)
    def _():
        carry[...] = jnp.zeros_like(carry)
        sweep([residual], inverse, adjoint, carry, work, planes, rows, True)
        pack_carry(adjoint, 0, send)


def adjoint_kernel(height, meta, residual, merged, beside, got, field, lower_adjoint, *rest):
    pieces, (adjoint, carry, *work) = rest[:MEMBERS], rest[MEMBERS:]
    planes, rows = residual.shape[0], residual.shape[2]
    margin = (rows - 2 * height) // 2
    upper = meta[2] == 0
    inverse = [merged.at[1], beside.at[1]]

    def products(adjoint):
        for k, piece in enumerate(pieces):
            who = meta[0] ^ k
            at_plane = (who // 2) * (planes // 2)
            at_row = pl.multiple_of((who % 2) * height + margin, 8)
            for p in range(planes // 2):
                total = 0.0
                for c in range(2):
                    total += (
                        field[at_plane + p, c, pl.ds(at_row, height), :LANES]
                        * adjoint[at_plane + p, c, pl.ds(at_row, height), :LANES]
                    )
                piece[p] = total * (1.0 / MEMBERS)

    @pl.when(upper)
    def _():
        unpack_carry(got, carry)
        sweep([residual], inverse, adjoint, carry, work, planes, rows, True)
        products(adjoint)

    @pl.when(jnp.logical_not(upper))
    def _():
        products(lower_adjoint)


def field_kernel(meta, *refs):
    out = refs[MEMBERS]
    for k, piece in enumerate(refs[MEMBERS - 1 :: -1]):
        out[:, :, meta[0] ^ k] = piece[...]


def body(source, observed, wavenumber, damping):
    own_planes, _, shots, height, width = source.shape
    planes, high = 2 * own_planes, 2 * height
    one_group = lax.axis_size("gx") == 2
    rows = high if one_group else high + 2 * WIDE
    tile = (own_planes, 2, height, width)

    inverse = inverses(wavenumber, damping)
    far = call(
        lambda *refs: prepare_kernel(ACROSS, *refs), [(2, *tile)] * 2, source, inverse
    )
    near = call(
        lambda *refs: prepare_kernel(ALONG, *refs), [(2, *tile)] * 2, source, inverse, far[0]
    )
    sends = [*near, *far]
    observed, *sends = lax.optimization_barrier([observed, *sends])
    pieces = gathered(sends)
    seen_edges = call(observed_edges_kernel, [(2, height, width)] * 2, observed)
    seen_edges = neighbour_swaps(*seen_edges, "gy", 1, ring=True)
    shape = [(2 * own_planes + 1, height, width)] * 2
    far = call(lambda *refs: observed_sends_kernel(ACROSS, *refs), shape, observed, *seen_edges)
    near = call(
        lambda *refs: observed_sends_kernel(ALONG, *refs), shape, observed, *seen_edges, far[0]
    )
    first_seen, *seen_sends = *near, *far
    *pieces, first_seen = lax.optimization_barrier([*pieces, first_seen])
    seen_sends = [first_seen, *seen_sends]
    edge_shape = (2, 2, high, width)
    (second,) = call(second_edges_kernel, [edge_shape], *pieces)
    merged, first = call(
        merge_kernel, [(2, planes, 2, high, width), edge_shape], *pieces, second
    )
    if not one_group:
        merged, first, second = (with_row_halo(a, WIDE) for a in (merged, first, second))
    first, second = neighbour_swaps(first, second, "gy", 1, ring=True)
    seen = gathered(seen_sends)

    (centre,) = call(
        centre_kernel,
        [(2, rows, width)],
        merged,
        scratch=[VMEM((planes, 2, rows, width), F32), *sweep_scratch(rows, width)],
    )
    centre = depth_pair_swap(centre)

    whole = (planes, 2, rows, 2 * width)
    scratch = sweep_scratch(rows)
    beside, field, send = call(
        forward_kernel,
        [(2, planes, 2, rows, width), whole, (rows, width)],
        merged,
        second,
        first,
        scratch=scratch,
        cost=30_000_000,
    )
    got = depth_pair_swap(send)
    (seen,) = call(
        merge_observed_kernel, [(planes, 2, high, 2 * width)], *seen, cost=100_000_000
    )
    seen = seen if one_group else with_row_halo(seen, WIDE)
    field, residual, adjoint, send = call(
        turn_kernel,
        [whole, whole, whole, (2 * rows + rows // 4, width)],
        merged,
        beside,
        centre,
        got,
        seen,
        field,
        scratch=scratch,
    )
    got = depth_pair_swap(send)
    pieces = gathered(
        call(lambda *refs: cut_kernel(height, *refs), [tile] * MEMBERS, field, send)
    )
    sums = call(
        lambda *refs: adjoint_kernel(height, *refs),
        [(own_planes, height, width)] * MEMBERS,
        residual,
        merged,
        beside,
        got,
        field,
        adjoint,
        scratch=[VMEM(whole, F32), *scratch],
    )
    sums = gathered(sums)
    gradient = (sums[0] + sums[1]) + (sums[2] + sums[3])
    (forward_field,) = call(field_kernel, [source.shape], *pieces)
    return forward_field, gradient


def solution(mesh):
    lateral = P("depth", None, None, "gx", "gy")
    return jax.shard_map(
        body,
        mesh=mesh,
        in_specs=(lateral, lateral, P("depth", "gx", "gy"), P("depth", "gx", "gy")),
        out_specs=(lateral, P("depth", "gx", "gy")),
        check_vma=False,
    )
```

```python
import jax
import jax.numpy as jnp
from jax import lax
from jax.experimental import pallas as pl
from jax.experimental.pallas import tpu as pltpu
from jax.sharding import PartitionSpec as P

MEMBERS = 4
WIDE = 32
NARROW = 16
LANES = 128
ALONG, ACROSS = (0, 1), (2, 3)
REACH = 8
DOWN = 24

VMEM = pltpu.VMEM
F32 = jnp.float32


def lane_ids(shape):
    return lax.broadcasted_iota(jnp.int32, shape, len(shape) - 1)


def position():
    zi, xi, yi = (lax.axis_index(a) for a in ("depth", "gx", "gy"))
    outermost = (yi == 0) | (yi == lax.axis_size("gy") - 1)
    return 2 * (zi % 2) + xi % 2, yi % 2, zi // 2, outermost


def call(kernel, outs, *operands, scratch=(), cost=3_000_000):
    return pl.pallas_call(
        lambda *refs: kernel(position(), *refs),
        out_shape=[jax.ShapeDtypeStruct(shape, F32) for shape in outs],
        in_specs=[pl.BlockSpec(memory_space=VMEM)] * len(operands),
        out_specs=[pl.BlockSpec(memory_space=VMEM)] * len(outs),
        scratch_shapes=list(scratch),
        cost_estimate=pl.CostEstimate(flops=0, bytes_accessed=cost, transcendentals=0),
        compiler_params=pltpu.CompilerParams(vmem_limit_bytes=8 * 1024 * 1024),
    )(*operands)


def member_swap(block, offset):
    nz, nx = lax.axis_size("depth"), lax.axis_size("gx")
    dz, dx = offset >> 1, offset & 1
    pairs = [(z * nx + x, (z ^ dz) * nx + (x ^ dx)) for z in range(nz) for x in range(nx)]
    return lax.ppermute(block, ("depth", "gx"), pairs)


def gathered(sends):
    return [member_swap(sends[k], k) for k in (3, 2, 1)] + [sends[0]]


def depth_pair_swap(block):
    return lax.ppermute(block, "depth", [(z, z ^ 2) for z in range(lax.axis_size("depth"))])


def neighbour_swaps(first, second, axis, stride):
    size = lax.axis_size(axis)
    count = size // stride

    def pairs(start):
        found = []
        for low in range(start, count - 1, 2):
            for part in range(stride):
                a, b = low * stride + part, (low + 1) * stride + part
                found += [(a, b), (b, a)]
        return found

    got_second = lax.ppermute(second, axis, pairs(1)) if count > 2 else jnp.zeros_like(second)
    got_first = lax.ppermute(first, axis, pairs(0)) if count > 1 else jnp.zeros_like(first)
    return got_first, got_second


def side_swaps(first, second):
    nx, ny = lax.axis_size("gx"), lax.axis_size("gy")
    if ny % 2 or ny == 2:
        return neighbour_swaps(first, second, "gy", 1)
    pairs = []
    for x in range(nx):
        for low in range(1, ny - 1, 2):
            a, b = x * ny + low, x * ny + low + 1
            pairs += [(a, b), (b, a)]
        pairs += [(x * ny + end, (x ^ 1) * ny + end) for end in (0, ny - 1)]
    got_second = lax.ppermute(second, ("gx", "gy"), pairs)
    got_first = lax.ppermute(first, "gy", [(y, y ^ 1) for y in range(ny)])
    return got_first, got_second


def with_row_halo(block, width):
    groups = lax.axis_size("gx") // 2
    if groups == 1:
        return block
    even = (lax.axis_index("gx") // 2) % 2 == 0
    top, bottom = block[..., :width, :], block[..., -width:, :]
    one, two = neighbour_swaps(
        jnp.where(even, bottom, top), jnp.where(even, top, bottom), "gx", 2
    )
    above, below = jnp.where(even, two, one), jnp.where(even, one, two)
    return jnp.concatenate([above, block, below], axis=-2)


def merge_members(meta, pieces, out):
    me = meta[0]
    for k, piece in enumerate(pieces):
        fields, planes, _, rows, _ = piece.shape
        who = me ^ k
        at_plane = (who // 2) * planes
        at_row = pl.multiple_of((who % 2) * rows, rows)
        for f in range(fields):
            for p in range(planes):
                for c in range(2):
                    out[f, at_plane + p, c, pl.ds(at_row, rows), :] = piece[f, p, c]


def pack_edges(meta, pieces, width, first, out):
    me, even = meta[0], meta[1] == 0
    fields, planes, _, rows, count = pieces[0].shape
    lanes = lane_ids((rows, count))

    def pack(lower, right):
        for k in range(2):
            strip = pl.ds(pl.multiple_of(((me ^ k) % 2) * rows, rows), rows)
            pair = (pieces[k + 2], pieces[k]) if lower else (pieces[k], pieces[k + 2])
            for f in range(fields):
                for c in range(2):
                    side = None
                    for j in range(2 * planes):
                        got = pair[j // planes][f, j % planes, c]
                        turn = (j * width + (width if right else 0)) % count
                        got = pltpu.roll(got, turn, 1) if turn else got
                        side = got if j == 0 else jnp.where(lanes >= j * width, got, side)
                    out[f, c, strip, :] = side

    for lower in (False, True):
        for right in (False, True):
            pl.when(((me >= 2) == lower) & ((even == first) == right))(
                lambda lower=lower, right=right: pack(lower, right)
            )


def beside_tile(right, right_turn, left, left_turn, width):
    lanes = lane_ids(right.shape)
    right = pltpu.roll(right, right_turn, 1) if right_turn else right
    left = pltpu.roll(left, left_turn, 1) if left_turn else left
    return jnp.where(lanes < width, right, jnp.where(lanes >= LANES - width, left, 0.0))


def edge_lanes(shape, margin):
    lanes = lane_ids(shape)
    return (lanes < margin) | (lanes >= LANES - margin)


def slot_lanes(shape, block):
    return lax.rem(lane_ids(shape) + (LANES - 16 * block - LANES // 2 + 8), LANES // 2) < 16


def folded_edges(field, at):
    real, imag = field[at, 0, :, LANES:], field[at, 1, :, LANES:]
    return jnp.where(edge_lanes(real.shape, WIDE), real, pltpu.roll(imag, LANES // 2, 1))


def pack_sides(field, at, out):
    packed = folded_edges(field, at)
    lanes = lane_ids(packed.shape)
    for c, gap in enumerate((DOWN, DOWN + LANES // 2)):
        centre = field[at, c, :, :LANES]
        near, far = pltpu.roll(centre, gap, 1), pltpu.roll(centre, gap + 2 * REACH, 1)
        packed = jnp.where((lanes >= gap) & (lanes < gap + REACH), near, packed)
        packed = jnp.where((lanes >= gap + REACH) & (lanes < gap + 2 * REACH), far, packed)
    out[...] = packed


def unpack_sides(centre, sides, out):
    packed = sides[...]
    lanes = lane_ids(packed.shape)
    keep = edge_lanes(packed.shape, DOWN)
    for c, gap in enumerate((DOWN, DOWN + LANES // 2)):
        near = pltpu.roll(packed, LANES - gap, 1)
        far = pltpu.roll(packed, LANES - gap - 2 * REACH, 1)
        out[c, :, :LANES] = jnp.where(
            lanes < REACH, near, jnp.where(lanes >= LANES - REACH, far, centre[c])
        )
        edges = pltpu.roll(packed, LANES // 2, 1) if c else packed
        out[c, :, LANES:] = jnp.where(keep, edges, 0.0)


def pack_carry(field, at, out):
    rows = field.shape[2]
    out[:rows] = field[at, 0, :, :LANES]
    out[rows : 2 * rows] = field[at, 1, :, :LANES]
    edges = folded_edges(field, at)
    part = rows // 4
    packed = edges[:part]
    for b in range(1, 4):
        turned = pltpu.roll(edges[b * part : (b + 1) * part], 16 * b, 1)
        packed = jnp.where(slot_lanes(packed.shape, b), turned, packed)
    out[2 * rows :] = packed


def unpack_carry(packed, out):
    rows = out.shape[1]
    quarter = packed[2 * rows :]
    edges = jnp.concatenate(
        [pltpu.roll(quarter, LANES - 16 * b, 1) if b else quarter for b in range(4)], axis=0
    )
    keep = edge_lanes(edges.shape, 8)
    for c in range(2):
        out[c, :, :LANES] = packed[c * rows : (c + 1) * rows]
        out[c, :, LANES:] = jnp.where(keep, pltpu.roll(edges, LANES // 2, 1) if c else edges, 0.0)


def times(a, b, q_real, q_imag, sign):
    if sign > 0:
        return a * q_real - b * q_imag, a * q_imag + b * q_real
    return a * q_real + b * q_imag, b * q_real - a * q_imag


def beside_each_other(refs):
    def read(z, c, strip):
        parts = [ref[z, c, strip, :] for ref in refs]
        return parts[0] if len(parts) == 1 else jnp.concatenate(parts, axis=1)

    return read


def sweep(drive, inverse, out, carry, work, planes, rows, reverse):
    drive, inverse = beside_each_other(drive), beside_each_other(inverse)
    rhs, ping, pong = work
    sign = -1 if reverse else 1
    width = out.shape[-1]
    zeros = jnp.zeros((8, width), F32)
    for buffer in (ping, pong):
        for c in range(2):
            buffer[c, :8, :] = zeros
            buffer[c, rows + 8 : rows + 16, :] = zeros

    def beside(buffer, c, r):
        here = buffer[c, r + 8 : r + 16, :]
        return (
            buffer[c, r + 7 : r + 15, :]
            + buffer[c, r + 9 : r + 17, :]
            + (pltpu.roll(here, 1, 1) + pltpu.roll(here, width - 1, 1))
        )

    def plane(step, _):
        z = planes - 1 - step if reverse else step
        for r in range(0, rows, 8):
            strip = slice(r, r + 8)
            a = drive(z, 0, strip) + 2.5 * carry[0, strip, :]
            b = drive(z, 1, strip) + 2.5 * carry[1, strip, :]
            rhs[0, strip, :] = a
            rhs[1, strip, :] = b
            a, b = times(a, b, inverse(z, 0, strip), inverse(z, 1, strip), sign)
            ping[0, r + 8 : r + 16, :] = a
            ping[1, r + 8 : r + 16, :] = b
        for r in range(0, rows, 8):
            strip = slice(r, r + 8)
            a = rhs[0, strip, :] + beside(ping, 0, r)
            b = rhs[1, strip, :] + beside(ping, 1, r)
            a, b = times(a, b, inverse(z, 0, strip), inverse(z, 1, strip), sign)
            pong[0, r + 8 : r + 16, :] = a
            pong[1, r + 8 : r + 16, :] = b
        for r in range(0, rows, 8):
            strip = slice(r, r + 8)
            a = rhs[0, strip, :] + beside(pong, 0, r)
            b = rhs[1, strip, :] + beside(pong, 1, r)
            a, b = times(a, b, inverse(z, 0, strip), inverse(z, 1, strip), sign)
            out[z, 0, strip, :] = a
            out[z, 1, strip, :] = b
            carry[0, strip, :] = a
            carry[1, strip, :] = b
        return 0

    lax.fori_loop(0, planes, plane, 0)


def sweep_scratch(rows, wide=2 * LANES):
    return [
        VMEM((2, rows, wide), F32),
        VMEM((2, rows, wide), F32),
        VMEM((2, rows + 16, wide), F32),
        VMEM((2, rows + 16, wide), F32),
    ]


def inverses(wavenumber, damping):
    real_diag = 6.0 - wavenumber
    denom = real_diag * real_diag + damping * damping
    return jnp.stack([real_diag / denom, -(damping / denom)], axis=1)


def edges_kernel(first, meta, *refs):
    pack_edges(meta, refs[MEMBERS - 1 :: -1], WIDE, first, refs[-1])


def merge_kernel(meta, *refs):
    merge_members(meta, refs[MEMBERS - 1 :: -1], refs[MEMBERS])


def prepare_kernel(ks, meta, source, inverse, *refs):
    for k, send in zip(ks, refs[-len(ks) :]):
        send[0] = source[:, :, meta[0] ^ k]
        send[1] = inverse[...]


def observed_edges_kernel(meta, observed, first, second):
    even = meta[1] == 0
    planes, _, shots, rows, count = observed.shape
    lanes = lane_ids((rows, count))
    per_tile = count // NARROW
    sides = {}
    for s in range(shots):
        for p in range(planes):
            for c in range(2):
                tile, j = divmod((s * planes + p) * 2 + c, per_tile)
                at = j * NARROW
                block = observed[p, c, s]
                for side, turn in (("left", at), ("right", (at + NARROW) % count)):
                    got = pltpu.roll(block, turn, 1) if turn else block
                    if j:
                        got = jnp.where(lanes >= at, got, sides[side])
                    sides[side] = got
                if j == per_tile - 1:
                    first[tile] = jnp.where(even, sides["right"], sides["left"])
                    second[tile] = jnp.where(even, sides["left"], sides["right"])


def observed_sends_kernel(ks, meta, observed, first, second, *refs):
    even = meta[1] == 0
    planes, _, _, rows, count = observed.shape
    lanes = lane_ids((rows, count))
    for k, send in zip(ks, refs[-len(ks) :]):
        shot = meta[0] ^ k
        for p in range(planes):
            for c in range(2):
                send[2 * p + c] = observed[p, c, shot]
        one, two = first[shot // 2], second[shot // 2]
        right, left = jnp.where(even, one, two), jnp.where(even, two, one)
        odd = lax.rem(shot, 2)
        right = pltpu.roll(right, odd * (count // 2), 1)
        left = pltpu.roll(left, (1 - odd) * (count // 2), 1)
        send[2 * planes] = jnp.where(lanes < count // 2, right, left)


def merge_observed_kernel(meta, *refs):
    pieces, out = refs[MEMBERS - 1 :: -1], refs[-1]
    planes = out.shape[0] // 2
    _, rows, count = pieces[0].shape
    for k, piece in enumerate(pieces):
        who = meta[0] ^ k
        at_plane = (who // 2) * planes
        strip = pl.ds(pl.multiple_of((who % 2) * rows, rows), rows)
        edges = piece[2 * planes]
        for p in range(planes):
            for c in range(2):
                at = (2 * p + c) * NARROW
                out[at_plane + p, c, strip, :LANES] = piece[2 * p + c]
                out[at_plane + p, c, strip, LANES:] = beside_tile(
                    edges,
                    (count - at) % count,
                    edges,
                    (count // 2 - NARROW - at) % count,
                    NARROW,
                )


def centre_kernel(meta, merged, send, field, carry, *work):
    planes, rows = merged.shape[1], merged.shape[3]

    @pl.when(meta[2] == 0)
    def _():
        carry[...] = jnp.zeros_like(carry)
        sweep([merged.at[0]], [merged.at[1]], field, carry, work, planes, rows, False)
        send[...] = carry[...]


def forward_kernel(meta, merged, second, first, sides, field, send, carry, *work):
    planes, rows = merged.shape[1], merged.shape[3]
    even, alone = meta[1] == 0, meta[3]
    for f in range(2):
        for c in range(2):
            for r in range(0, rows, 32):
                strip = slice(r, r + 32)
                one, two = first[f, c, strip, :], second[f, c, strip, :]
                two = jnp.where(alone, 0.0, two) if f else two
                right, left = jnp.where(even, one, two), jnp.where(even, two, one)
                for p in range(planes):
                    at = p * WIDE
                    sides[f, p, c, strip, :] = beside_tile(
                        right, (LANES - at) % LANES, left, (2 * LANES - WIDE - at) % LANES, WIDE
                    )

    @pl.when(meta[2] == 0)
    def _():
        carry[...] = jnp.zeros_like(carry)
        drive, inverse = ([merged.at[f], sides.at[f]] for f in range(2))
        sweep(drive, inverse, field, carry, work, planes, rows, False)
        pack_sides(field, planes - 1, send)


def cut_kernel(height, meta, field, _, *pieces):
    planes, rows = field.shape[0], field.shape[2]
    margin = (rows - 2 * height) // 2
    for k, piece in enumerate(pieces):
        who = meta[0] ^ k
        at_plane = (who // 2) * (planes // 2)
        at_row = pl.multiple_of((who % 2) * height + margin, 8)
        for p in range(planes // 2):
            for c in range(2):
                piece[p, c] = field[at_plane + p, c, pl.ds(at_row, height), :LANES]


def turn_kernel(
    meta,
    merged,
    beside,
    centre,
    sides,
    observed,
    upper_field,
    field,
    residual,
    adjoint,
    send,
    carry,
    *work,
):
    planes, rows = merged.shape[1], merged.shape[3]
    drive, inverse = ([merged.at[f], beside.at[f]] for f in range(2))
    lower = meta[2] == 1

    @pl.when(jnp.logical_not(lower))
    def _():
        field[...] = upper_field[...]

    @pl.when(lower)
    def _():
        unpack_sides(centre, sides, carry)
        sweep(drive, inverse, field, carry, work, planes, rows, False)

    residual[...] = field[...] - observed[...]

    @pl.when(lower)
    def _():
        carry[...] = jnp.zeros_like(carry)
        sweep([residual], inverse, adjoint, carry, work, planes, rows, True)
        pack_carry(adjoint, 0, send)


def adjoint_kernel(height, meta, residual, merged, beside, got, field, lower_adjoint, *rest):
    pieces, (adjoint, carry, *work) = rest[:MEMBERS], rest[MEMBERS:]
    planes, rows = residual.shape[0], residual.shape[2]
    margin = (rows - 2 * height) // 2
    upper = meta[2] == 0
    inverse = [merged.at[1], beside.at[1]]

    def products(adjoint):
        for k, piece in enumerate(pieces):
            who = meta[0] ^ k
            at_plane = (who // 2) * (planes // 2)
            at_row = pl.multiple_of((who % 2) * height + margin, 8)
            for p in range(planes // 2):
                total = 0.0
                for c in range(2):
                    total += (
                        field[at_plane + p, c, pl.ds(at_row, height), :LANES]
                        * adjoint[at_plane + p, c, pl.ds(at_row, height), :LANES]
                    )
                piece[p] = total * (1.0 / MEMBERS)

    @pl.when(upper)
    def _():
        unpack_carry(got, carry)
        sweep([residual], inverse, adjoint, carry, work, planes, rows, True)
        products(adjoint)

    @pl.when(jnp.logical_not(upper))
    def _():
        products(lower_adjoint)


def field_kernel(meta, *refs):
    out = refs[MEMBERS]
    for k, piece in enumerate(refs[MEMBERS - 1 :: -1]):
        out[:, :, meta[0] ^ k] = piece[...]


def body(source, observed, wavenumber, damping):
    own_planes, _, shots, height, width = source.shape
    planes, high = 2 * own_planes, 2 * height
    one_group = lax.axis_size("gx") == 2
    rows = high if one_group else high + 2 * WIDE
    tile = (own_planes, 2, height, width)

    inverse = inverses(wavenumber, damping)
    far = call(
        lambda *refs: prepare_kernel(ACROSS, *refs), [(2, *tile)] * 2, source, inverse
    )
    near = call(
        lambda *refs: prepare_kernel(ALONG, *refs), [(2, *tile)] * 2, source, inverse, far[0]
    )
    sends = [*near, *far]
    observed, *sends = lax.optimization_barrier([observed, *sends])
    pieces = gathered(sends)
    seen_edges = call(observed_edges_kernel, [(2, height, width)] * 2, observed)
    seen_edges = side_swaps(*seen_edges)
    *pieces, one, two = lax.optimization_barrier([*pieces, *seen_edges])
    edge_shape = (2, 2, high, width)
    (second,) = call(lambda *refs: edges_kernel(False, *refs), [edge_shape], *pieces)
    (merged,) = call(merge_kernel, [(2, planes, 2, high, width)], *pieces)
    if not one_group:
        merged = with_row_halo(merged, WIDE)
    (centre,) = call(
        centre_kernel,
        [(2, rows, width)],
        merged,
        scratch=[VMEM((planes, 2, rows, width), F32), *sweep_scratch(rows, width)],
    )
    (first,) = call(lambda *refs: edges_kernel(True, *refs), [edge_shape], *pieces, centre)
    packed = first
    if not one_group:
        first, second = (with_row_halo(a, WIDE) for a in (first, second))
    first, second = side_swaps(first, second)
    centre = depth_pair_swap(centre)
    shape = [(2 * own_planes + 1, height, width)] * 2
    far = call(lambda *refs: observed_sends_kernel(ACROSS, *refs), shape, observed, one, two, packed)
    near = call(
        lambda *refs: observed_sends_kernel(ALONG, *refs), shape, observed, one, two, far[0]
    )
    seen = gathered([*near, *far])

    whole = (planes, 2, rows, 2 * width)
    scratch = sweep_scratch(rows)
    beside, field, send = call(
        forward_kernel,
        [(2, planes, 2, rows, width), whole, (rows, width)],
        merged,
        second,
        first,
        scratch=scratch,
        cost=30_000_000,
    )
    got = depth_pair_swap(send)
    (seen,) = call(
        merge_observed_kernel, [(planes, 2, high, 2 * width)], *seen, centre, cost=3_000_000
    )
    seen = seen if one_group else with_row_halo(seen, WIDE)
    field, residual, adjoint, send = call(
        turn_kernel,
        [whole, whole, whole, (2 * rows + rows // 4, width)],
        merged,
        beside,
        centre,
        got,
        seen,
        field,
        scratch=scratch,
    )
    got = depth_pair_swap(send)
    pieces = gathered(
        call(lambda *refs: cut_kernel(height, *refs), [tile] * MEMBERS, field, send)
    )
    sums = call(
        lambda *refs: adjoint_kernel(height, *refs),
        [(own_planes, height, width)] * MEMBERS,
        residual,
        merged,
        beside,
        got,
        field,
        adjoint,
        scratch=[VMEM(whole, F32), *scratch],
    )
    sums = gathered(sums)
    gradient = (sums[0] + sums[1]) + (sums[2] + sums[3])
    (forward_field,) = call(field_kernel, [source.shape], *pieces)
    return forward_field, gradient


def solution(mesh):
    lateral = P("depth", None, None, "gx", "gy")
    return jax.shard_map(
        body,
        mesh=mesh,
        in_specs=(lateral, lateral, P("depth", "gx", "gy"), P("depth", "gx", "gy")),
        out_specs=(lateral, P("depth", "gx", "gy")),
        check_vma=False,
    )
```

```python
import jax
import jax.numpy as jnp
from jax import lax
from jax.experimental import pallas as pl
from jax.experimental.pallas import tpu as pltpu
from jax.sharding import PartitionSpec as P

MEMBERS = 4
WIDE = 32
NARROW = 16
LANES = 128
ALONG, ACROSS = (0, 1), (2, 3)
REACH = 8
DOWN = 24

VMEM = pltpu.VMEM
F32 = jnp.float32


def lane_ids(shape):
    return lax.broadcasted_iota(jnp.int32, shape, len(shape) - 1)


def position():
    zi, xi, yi = (lax.axis_index(a) for a in ("depth", "gx", "gy"))
    outermost = (yi == 0) | (yi == lax.axis_size("gy") - 1)
    return 2 * (zi % 2) + xi % 2, yi % 2, zi // 2, outermost


def call(kernel, outs, *operands, scratch=(), cost=3_000_000):
    return pl.pallas_call(
        lambda *refs: kernel(position(), *refs),
        out_shape=[jax.ShapeDtypeStruct(shape, F32) for shape in outs],
        in_specs=[pl.BlockSpec(memory_space=VMEM)] * len(operands),
        out_specs=[pl.BlockSpec(memory_space=VMEM)] * len(outs),
        scratch_shapes=list(scratch),
        cost_estimate=pl.CostEstimate(flops=0, bytes_accessed=cost, transcendentals=0),
        compiler_params=pltpu.CompilerParams(vmem_limit_bytes=8 * 1024 * 1024),
    )(*operands)


def member_swap(block, offset):
    nz, nx = lax.axis_size("depth"), lax.axis_size("gx")
    dz, dx = offset >> 1, offset & 1
    pairs = [(z * nx + x, (z ^ dz) * nx + (x ^ dx)) for z in range(nz) for x in range(nx)]
    return lax.ppermute(block, ("depth", "gx"), pairs)


def gathered(sends):
    return [member_swap(sends[k], k) for k in (3, 2, 1)] + [sends[0]]


def depth_pair_swap(block):
    return lax.ppermute(block, "depth", [(z, z ^ 2) for z in range(lax.axis_size("depth"))])


def neighbour_swaps(first, second, axis, stride):
    size = lax.axis_size(axis)
    count = size // stride

    def pairs(start):
        found = []
        for low in range(start, count - 1, 2):
            for part in range(stride):
                a, b = low * stride + part, (low + 1) * stride + part
                found += [(a, b), (b, a)]
        return found

    got_second = lax.ppermute(second, axis, pairs(1)) if count > 2 else jnp.zeros_like(second)
    got_first = lax.ppermute(first, axis, pairs(0)) if count > 1 else jnp.zeros_like(first)
    return got_first, got_second


def side_swaps(first, second):
    nx, ny = lax.axis_size("gx"), lax.axis_size("gy")
    if ny % 2 or ny == 2:
        return neighbour_swaps(first, second, "gy", 1)
    pairs = []
    for x in range(nx):
        for low in range(1, ny - 1, 2):
            a, b = x * ny + low, x * ny + low + 1
            pairs += [(a, b), (b, a)]
        pairs += [(x * ny + end, (x ^ 1) * ny + end) for end in (0, ny - 1)]
    got_second = lax.ppermute(second, ("gx", "gy"), pairs)
    got_first = lax.ppermute(first, "gy", [(y, y ^ 1) for y in range(ny)])
    return got_first, got_second


def with_row_halo(block, width):
    groups = lax.axis_size("gx") // 2
    if groups == 1:
        return block
    even = (lax.axis_index("gx") // 2) % 2 == 0
    top, bottom = block[..., :width, :], block[..., -width:, :]
    one, two = neighbour_swaps(
        jnp.where(even, bottom, top), jnp.where(even, top, bottom), "gx", 2
    )
    above, below = jnp.where(even, two, one), jnp.where(even, one, two)
    return jnp.concatenate([above, block, below], axis=-2)


def merge_members(meta, pieces, out):
    me = meta[0]
    for k, piece in enumerate(pieces):
        fields, planes, _, rows, _ = piece.shape
        who = me ^ k
        at_plane = (who // 2) * planes
        at_row = pl.multiple_of((who % 2) * rows, rows)
        for f in range(fields):
            for p in range(planes):
                for c in range(2):
                    out[f, at_plane + p, c, pl.ds(at_row, rows), :] = piece[f, p, c]


def pack_edges(meta, pieces, width, first, out):
    me, even = meta[0], meta[1] == 0
    fields, planes, _, rows, count = pieces[0].shape
    lanes = lane_ids((rows, count))

    def pack(lower, right):
        for k in range(2):
            strip = pl.ds(pl.multiple_of(((me ^ k) % 2) * rows, rows), rows)
            pair = (pieces[k + 2], pieces[k]) if lower else (pieces[k], pieces[k + 2])
            for f in range(fields):
                for c in range(2):
                    side = None
                    for j in range(2 * planes):
                        got = pair[j // planes][f, j % planes, c]
                        turn = (j * width + (width if right else 0)) % count
                        got = pltpu.roll(got, turn, 1) if turn else got
                        side = got if j == 0 else jnp.where(lanes >= j * width, got, side)
                    out[f, c, strip, :] = side

    for lower in (False, True):
        for right in (False, True):
            pl.when(((me >= 2) == lower) & ((even == first) == right))(
                lambda lower=lower, right=right: pack(lower, right)
            )


def beside_tile(right, right_turn, left, left_turn, width):
    lanes = lane_ids(right.shape)
    right = pltpu.roll(right, right_turn, 1) if right_turn else right
    left = pltpu.roll(left, left_turn, 1) if left_turn else left
    return jnp.where(lanes < width, right, jnp.where(lanes >= LANES - width, left, 0.0))


def edge_lanes(shape, margin):
    lanes = lane_ids(shape)
    return (lanes < margin) | (lanes >= LANES - margin)


def slot_lanes(shape, block):
    return lax.rem(lane_ids(shape) + (LANES - 16 * block - LANES // 2 + 8), LANES // 2) < 16


def folded_edges(field, at):
    real, imag = field[at, 0, :, LANES:], field[at, 1, :, LANES:]
    return jnp.where(edge_lanes(real.shape, WIDE), real, pltpu.roll(imag, LANES // 2, 1))


def pack_sides(field, at, out):
    packed = folded_edges(field, at)
    lanes = lane_ids(packed.shape)
    for c, gap in enumerate((DOWN, DOWN + LANES // 2)):
        centre = field[at, c, :, :LANES]
        near, far = pltpu.roll(centre, gap, 1), pltpu.roll(centre, gap + 2 * REACH, 1)
        packed = jnp.where((lanes >= gap) & (lanes < gap + REACH), near, packed)
        packed = jnp.where((lanes >= gap + REACH) & (lanes < gap + 2 * REACH), far, packed)
    out[...] = packed


def unpack_sides(centre, sides, out):
    packed = sides[...]
    lanes = lane_ids(packed.shape)
    keep = edge_lanes(packed.shape, DOWN)
    for c, gap in enumerate((DOWN, DOWN + LANES // 2)):
        near = pltpu.roll(packed, LANES - gap, 1)
        far = pltpu.roll(packed, LANES - gap - 2 * REACH, 1)
        out[c, :, :LANES] = jnp.where(
            lanes < REACH, near, jnp.where(lanes >= LANES - REACH, far, centre[c])
        )
        edges = pltpu.roll(packed, LANES // 2, 1) if c else packed
        out[c, :, LANES:] = jnp.where(keep, edges, 0.0)


def pack_carry(field, at, out):
    rows = field.shape[2]
    out[:rows] = field[at, 0, :, :LANES]
    out[rows : 2 * rows] = field[at, 1, :, :LANES]
    edges = folded_edges(field, at)
    part = rows // 4
    packed = edges[:part]
    for b in range(1, 4):
        turned = pltpu.roll(edges[b * part : (b + 1) * part], 16 * b, 1)
        packed = jnp.where(slot_lanes(packed.shape, b), turned, packed)
    out[2 * rows :] = packed


def unpack_carry(packed, out):
    rows = out.shape[1]
    quarter = packed[2 * rows :]
    edges = jnp.concatenate(
        [pltpu.roll(quarter, LANES - 16 * b, 1) if b else quarter for b in range(4)], axis=0
    )
    keep = edge_lanes(edges.shape, 8)
    for c in range(2):
        out[c, :, :LANES] = packed[c * rows : (c + 1) * rows]
        out[c, :, LANES:] = jnp.where(keep, pltpu.roll(edges, LANES // 2, 1) if c else edges, 0.0)


def times(a, b, q_real, q_imag, sign):
    if sign > 0:
        return a * q_real - b * q_imag, a * q_imag + b * q_real
    return a * q_real + b * q_imag, b * q_real - a * q_imag


def beside_each_other(refs):
    def read(z, c, strip):
        parts = [ref[z, c, strip, :] for ref in refs]
        return parts[0] if len(parts) == 1 else jnp.concatenate(parts, axis=1)

    return read


def difference(one, two):
    return lambda z, c, strip: one[z, c, strip, :] - two[z, c, strip, :]


def sweep(drive, inverse, out, carry, work, planes, rows, reverse):
    drive = drive if callable(drive) else beside_each_other(drive)
    inverse = beside_each_other(inverse)
    rhs, ping, pong = work
    sign = -1 if reverse else 1
    width = out.shape[-1]
    zeros = jnp.zeros((8, width), F32)
    for buffer in (ping, pong):
        for c in range(2):
            buffer[c, :8, :] = zeros
            buffer[c, rows + 8 : rows + 16, :] = zeros

    def beside(buffer, c, r):
        here = buffer[c, r + 8 : r + 24, :]
        return (
            buffer[c, r + 7 : r + 23, :]
            + buffer[c, r + 9 : r + 25, :]
            + (pltpu.roll(here, 1, 1) + pltpu.roll(here, width - 1, 1))
        )

    def plane(step, _):
        z = planes - 1 - step if reverse else step
        for r in range(0, rows, 16):
            strip = slice(r, r + 16)
            a = drive(z, 0, strip) + 2.5 * carry[0, strip, :]
            b = drive(z, 1, strip) + 2.5 * carry[1, strip, :]
            rhs[0, strip, :] = a
            rhs[1, strip, :] = b
            a, b = times(a, b, inverse(z, 0, strip), inverse(z, 1, strip), sign)
            ping[0, r + 8 : r + 24, :] = a
            ping[1, r + 8 : r + 24, :] = b
        for r in range(0, rows, 16):
            strip = slice(r, r + 16)
            a = rhs[0, strip, :] + beside(ping, 0, r)
            b = rhs[1, strip, :] + beside(ping, 1, r)
            a, b = times(a, b, inverse(z, 0, strip), inverse(z, 1, strip), sign)
            pong[0, r + 8 : r + 24, :] = a
            pong[1, r + 8 : r + 24, :] = b
        for r in range(0, rows, 16):
            strip = slice(r, r + 16)
            a = rhs[0, strip, :] + beside(pong, 0, r)
            b = rhs[1, strip, :] + beside(pong, 1, r)
            a, b = times(a, b, inverse(z, 0, strip), inverse(z, 1, strip), sign)
            out[z, 0, strip, :] = a
            out[z, 1, strip, :] = b
            carry[0, strip, :] = a
            carry[1, strip, :] = b
        return 0

    lax.fori_loop(0, planes, plane, 0)


def sweep_scratch(rows, wide=2 * LANES):
    return [
        VMEM((2, rows, wide), F32),
        VMEM((2, rows, wide), F32),
        VMEM((2, rows + 16, wide), F32),
        VMEM((2, rows + 16, wide), F32),
    ]


def inverses(wavenumber, damping):
    real_diag = 6.0 - wavenumber
    denom = real_diag * real_diag + damping * damping
    return jnp.stack([real_diag / denom, -(damping / denom)], axis=1)


def edges_kernel(first, meta, *refs):
    pack_edges(meta, refs[MEMBERS - 1 :: -1], WIDE, first, refs[-1])


def merge_kernel(meta, *refs):
    merge_members(meta, refs[MEMBERS - 1 :: -1], refs[MEMBERS])


def prepare_kernel(ks, meta, source, inverse, *refs):
    for k, send in zip(ks, refs[-len(ks) :]):
        send[0] = source[:, :, meta[0] ^ k]
        send[1] = inverse[...]


def observed_edges_kernel(meta, observed, first, second):
    even = meta[1] == 0
    planes, _, shots, rows, count = observed.shape
    lanes = lane_ids((rows, count))
    per_tile = count // NARROW
    sides = {}
    for s in range(shots):
        for p in range(planes):
            for c in range(2):
                tile, j = divmod((s * planes + p) * 2 + c, per_tile)
                at = j * NARROW
                block = observed[p, c, s]
                for side, turn in (("left", at), ("right", (at + NARROW) % count)):
                    got = pltpu.roll(block, turn, 1) if turn else block
                    if j:
                        got = jnp.where(lanes >= at, got, sides[side])
                    sides[side] = got
                if j == per_tile - 1:
                    first[tile] = jnp.where(even, sides["right"], sides["left"])
                    second[tile] = jnp.where(even, sides["left"], sides["right"])


def observed_sends_kernel(ks, meta, observed, first, second, *refs):
    even = meta[1] == 0
    planes, _, _, rows, count = observed.shape
    lanes = lane_ids((rows, count))
    for k, send in zip(ks, refs[-len(ks) :]):
        shot = meta[0] ^ k
        for p in range(planes):
            for c in range(2):
                send[2 * p + c] = observed[p, c, shot]
        one, two = first[shot // 2], second[shot // 2]
        right, left = jnp.where(even, one, two), jnp.where(even, two, one)
        odd = lax.rem(shot, 2)
        right = pltpu.roll(right, odd * (count // 2), 1)
        left = pltpu.roll(left, (1 - odd) * (count // 2), 1)
        send[2 * planes] = jnp.where(lanes < count // 2, right, left)


def merge_observed_kernel(meta, *refs):
    pieces, out = refs[MEMBERS - 1 :: -1], refs[-1]
    planes = out.shape[0] // 2
    _, rows, count = pieces[0].shape
    for k, piece in enumerate(pieces):
        who = meta[0] ^ k
        at_plane = (who // 2) * planes
        strip = pl.ds(pl.multiple_of((who % 2) * rows, rows), rows)
        edges = piece[2 * planes]
        for p in range(planes):
            for c in range(2):
                at = (2 * p + c) * NARROW
                out[at_plane + p, c, strip, :LANES] = piece[2 * p + c]
                out[at_plane + p, c, strip, LANES:] = beside_tile(
                    edges,
                    (count - at) % count,
                    edges,
                    (count // 2 - NARROW - at) % count,
                    NARROW,
                )


def centre_kernel(meta, merged, send, field, carry, *work):
    planes, rows = merged.shape[1], merged.shape[3]

    @pl.when(meta[2] == 0)
    def _():
        carry[...] = jnp.zeros_like(carry)
        sweep([merged.at[0]], [merged.at[1]], field, carry, work, planes, rows, False)
        send[...] = carry[...]


def forward_kernel(meta, merged, second, first, sides, field, send, carry, *work):
    planes, rows = merged.shape[1], merged.shape[3]
    even, alone = meta[1] == 0, meta[3]
    for f in range(2):
        for c in range(2):
            for r in range(0, rows, 32):
                strip = slice(r, r + 32)
                one, two = first[f, c, strip, :], second[f, c, strip, :]
                two = jnp.where(alone, 0.0, two) if f else two
                right, left = jnp.where(even, one, two), jnp.where(even, two, one)
                for p in range(planes):
                    at = p * WIDE
                    sides[f, p, c, strip, :] = beside_tile(
                        right, (LANES - at) % LANES, left, (2 * LANES - WIDE - at) % LANES, WIDE
                    )

    @pl.when(meta[2] == 0)
    def _():
        carry[...] = jnp.zeros_like(carry)
        drive, inverse = ([merged.at[f], sides.at[f]] for f in range(2))
        sweep(drive, inverse, field, carry, work, planes, rows, False)
        pack_sides(field, planes - 1, send)


def cut_kernel(height, meta, field, _, *pieces):
    planes, rows = field.shape[0], field.shape[2]
    margin = (rows - 2 * height) // 2
    for k, piece in enumerate(pieces):
        who = meta[0] ^ k
        at_plane = (who // 2) * (planes // 2)
        at_row = pl.multiple_of((who % 2) * height + margin, 8)
        for p in range(planes // 2):
            for c in range(2):
                piece[p, c] = field[at_plane + p, c, pl.ds(at_row, height), :LANES]


def turn_kernel(
    meta,
    merged,
    beside,
    centre,
    sides,
    observed,
    upper_field,
    field,
    adjoint,
    send,
    carry,
    *work,
):
    planes, rows = merged.shape[1], merged.shape[3]
    drive, inverse = ([merged.at[f], beside.at[f]] for f in range(2))
    lower = meta[2] == 1

    @pl.when(jnp.logical_not(lower))
    def _():
        field[...] = upper_field[...]

    @pl.when(lower)
    def _():
        unpack_sides(centre, sides, carry)
        sweep(drive, inverse, field, carry, work, planes, rows, False)
        carry[...] = jnp.zeros_like(carry)
        sweep(difference(field, observed), inverse, adjoint, carry, work, planes, rows, True)
        pack_carry(adjoint, 0, send)


def adjoint_kernel(height, meta, observed, merged, beside, got, field, lower_adjoint, *rest):
    pieces, (adjoint, carry, *work) = rest[:MEMBERS], rest[MEMBERS:]
    planes, rows = field.shape[0], field.shape[2]
    margin = (rows - 2 * height) // 2
    upper = meta[2] == 0
    inverse = [merged.at[1], beside.at[1]]

    def products(adjoint):
        for k, piece in enumerate(pieces):
            who = meta[0] ^ k
            at_plane = (who // 2) * (planes // 2)
            at_row = pl.multiple_of((who % 2) * height + margin, 8)
            for p in range(planes // 2):
                total = 0.0
                for c in range(2):
                    total += (
                        field[at_plane + p, c, pl.ds(at_row, height), :LANES]
                        * adjoint[at_plane + p, c, pl.ds(at_row, height), :LANES]
                    )
                piece[p] = total * (1.0 / MEMBERS)

    @pl.when(upper)
    def _():
        unpack_carry(got, carry)
        sweep(difference(field, observed), inverse, adjoint, carry, work, planes, rows, True)
        products(adjoint)

    @pl.when(jnp.logical_not(upper))
    def _():
        products(lower_adjoint)


def sum_kernel(meta, one, two, three, four, out):
    out[...] = (one[...] + two[...]) + (three[...] + four[...])


def field_kernel(meta, *refs):
    out = refs[MEMBERS]
    for k, piece in enumerate(refs[MEMBERS - 1 :: -1]):
        out[:, :, meta[0] ^ k] = piece[...]


def body(source, observed, wavenumber, damping):
    own_planes, _, shots, height, width = source.shape
    planes, high = 2 * own_planes, 2 * height
    one_group = lax.axis_size("gx") == 2
    rows = high if one_group else high + 2 * WIDE
    tile = (own_planes, 2, height, width)

    inverse = inverses(wavenumber, damping)
    far = call(
        lambda *refs: prepare_kernel(ACROSS, *refs), [(2, *tile)] * 2, source, inverse
    )
    near = call(
        lambda *refs: prepare_kernel(ALONG, *refs), [(2, *tile)] * 2, source, inverse, far[0]
    )
    sends = [*near, *far]
    observed, *sends = lax.optimization_barrier([observed, *sends])
    pieces = gathered(sends)
    seen_edges = call(observed_edges_kernel, [(2, height, width)] * 2, observed)
    seen_edges = side_swaps(*seen_edges)
    *pieces, one, two = lax.optimization_barrier([*pieces, *seen_edges])
    edge_shape = (2, 2, high, width)
    (second,) = call(lambda *refs: edges_kernel(False, *refs), [edge_shape], *pieces)
    (merged,) = call(merge_kernel, [(2, planes, 2, high, width)], *pieces)
    if not one_group:
        merged = with_row_halo(merged, WIDE)
    (centre,) = call(
        centre_kernel,
        [(2, rows, width)],
        merged,
        scratch=[VMEM((planes, 2, rows, width), F32), *sweep_scratch(rows, width)],
    )
    (first,) = call(lambda *refs: edges_kernel(True, *refs), [edge_shape], *pieces, centre)
    packed = first
    if not one_group:
        first, second = (with_row_halo(a, WIDE) for a in (first, second))
    first, second = side_swaps(first, second)
    centre = depth_pair_swap(centre)
    shape = [(2 * own_planes + 1, height, width)] * 2
    far = call(lambda *refs: observed_sends_kernel(ACROSS, *refs), shape, observed, one, two, packed)
    near = call(
        lambda *refs: observed_sends_kernel(ALONG, *refs), shape, observed, one, two, far[0]
    )
    seen = gathered([*near, *far])

    whole = (planes, 2, rows, 2 * width)
    scratch = sweep_scratch(rows)
    beside, field, send = call(
        forward_kernel,
        [(2, planes, 2, rows, width), whole, (rows, width)],
        merged,
        second,
        first,
        scratch=scratch,
        cost=30_000_000,
    )
    got = depth_pair_swap(send)
    (seen,) = call(
        merge_observed_kernel, [(planes, 2, high, 2 * width)], *seen, centre, cost=3_000_000
    )
    seen = seen if one_group else with_row_halo(seen, WIDE)
    field, adjoint, send = call(
        turn_kernel,
        [whole, whole, (2 * rows + rows // 4, width)],
        merged,
        beside,
        centre,
        got,
        seen,
        field,
        scratch=scratch,
    )
    got = depth_pair_swap(send)
    pieces = gathered(
        call(lambda *refs: cut_kernel(height, *refs), [tile] * MEMBERS, field, send)
    )
    sums = call(
        lambda *refs: adjoint_kernel(height, *refs),
        [(own_planes, height, width)] * MEMBERS,
        seen,
        merged,
        beside,
        got,
        field,
        adjoint,
        scratch=[VMEM(whole, F32), *scratch],
    )
    sums = gathered(sums)
    (gradient,) = call(sum_kernel, [wavenumber.shape], *sums)
    (forward_field,) = call(field_kernel, [source.shape], *pieces)
    return forward_field, gradient


def solution(mesh):
    lateral = P("depth", None, None, "gx", "gy")
    return jax.shard_map(
        body,
        mesh=mesh,
        in_specs=(lateral, lateral, P("depth", "gx", "gy"), P("depth", "gx", "gy")),
        out_specs=(lateral, P("depth", "gx", "gy")),
        check_vma=False,
    )
```

```python
import jax
import jax.numpy as jnp
from jax import lax
from jax.experimental import pallas as pl
from jax.experimental.pallas import tpu as pltpu
from jax.sharding import PartitionSpec as P

MEMBERS = 4
WIDE = 32
NARROW = 16
LANES = 128
ALONG, ACROSS = (0, 1), (2, 3)
REACH = 8
DOWN = 24

VMEM = pltpu.VMEM
F32 = jnp.float32


def lane_ids(shape):
    return lax.broadcasted_iota(jnp.int32, shape, len(shape) - 1)


def position():
    zi, xi, yi = (lax.axis_index(a) for a in ("depth", "gx", "gy"))
    outermost = (yi == 0) | (yi == lax.axis_size("gy") - 1)
    return 2 * (zi % 2) + xi % 2, yi % 2, zi // 2, outermost


def call(kernel, outs, *operands, scratch=(), cost=3_000_000):
    return pl.pallas_call(
        lambda *refs: kernel(position(), *refs),
        out_shape=[jax.ShapeDtypeStruct(shape, F32) for shape in outs],
        in_specs=[pl.BlockSpec(memory_space=VMEM)] * len(operands),
        out_specs=[pl.BlockSpec(memory_space=VMEM)] * len(outs),
        scratch_shapes=list(scratch),
        cost_estimate=pl.CostEstimate(flops=0, bytes_accessed=cost, transcendentals=0),
        compiler_params=pltpu.CompilerParams(vmem_limit_bytes=8 * 1024 * 1024),
    )(*operands)


def member_swap(block, offset):
    nz, nx = lax.axis_size("depth"), lax.axis_size("gx")
    dz, dx = offset >> 1, offset & 1
    pairs = [(z * nx + x, (z ^ dz) * nx + (x ^ dx)) for z in range(nz) for x in range(nx)]
    return lax.ppermute(block, ("depth", "gx"), pairs)


def gathered(sends):
    return [member_swap(sends[k], k) for k in (3, 2, 1)] + [sends[0]]


def depth_pair_swap(block):
    return lax.ppermute(block, "depth", [(z, z ^ 2) for z in range(lax.axis_size("depth"))])


def neighbour_swaps(first, second, axis, stride):
    size = lax.axis_size(axis)
    count = size // stride

    def pairs(start):
        found = []
        for low in range(start, count - 1, 2):
            for part in range(stride):
                a, b = low * stride + part, (low + 1) * stride + part
                found += [(a, b), (b, a)]
        return found

    got_second = lax.ppermute(second, axis, pairs(1)) if count > 2 else jnp.zeros_like(second)
    got_first = lax.ppermute(first, axis, pairs(0)) if count > 1 else jnp.zeros_like(first)
    return got_first, got_second


def side_swaps(first, second):
    nx, ny = lax.axis_size("gx"), lax.axis_size("gy")
    if ny % 2 or ny == 2:
        return neighbour_swaps(first, second, "gy", 1)
    pairs = []
    for x in range(nx):
        for low in range(1, ny - 1, 2):
            a, b = x * ny + low, x * ny + low + 1
            pairs += [(a, b), (b, a)]
        pairs += [(x * ny + end, (x ^ 1) * ny + end) for end in (0, ny - 1)]
    got_second = lax.ppermute(second, ("gx", "gy"), pairs)
    got_first = lax.ppermute(first, "gy", [(y, y ^ 1) for y in range(ny)])
    return got_first, got_second


def with_row_halo(block, width):
    groups = lax.axis_size("gx") // 2
    if groups == 1:
        return block
    even = (lax.axis_index("gx") // 2) % 2 == 0
    top, bottom = block[..., :width, :], block[..., -width:, :]
    one, two = neighbour_swaps(
        jnp.where(even, bottom, top), jnp.where(even, top, bottom), "gx", 2
    )
    above, below = jnp.where(even, two, one), jnp.where(even, one, two)
    return jnp.concatenate([above, block, below], axis=-2)


def merge_members(meta, pieces, out):
    me = meta[0]
    for k, piece in enumerate(pieces):
        fields, planes, _, rows, _ = piece.shape
        who = me ^ k
        at_plane = (who // 2) * planes
        at_row = pl.multiple_of((who % 2) * rows, rows)
        for f in range(fields):
            for p in range(planes):
                for c in range(2):
                    out[f, at_plane + p, c, pl.ds(at_row, rows), :] = piece[f, p, c]


def pack_edges(meta, pieces, width, first, out):
    me, even = meta[0], meta[1] == 0
    fields, planes, _, rows, count = pieces[0].shape
    lanes = lane_ids((rows, count))

    def pack(lower, right):
        for k in range(2):
            strip = pl.ds(pl.multiple_of(((me ^ k) % 2) * rows, rows), rows)
            pair = (pieces[k + 2], pieces[k]) if lower else (pieces[k], pieces[k + 2])
            for f in range(fields):
                for c in range(2):
                    side = None
                    for j in range(2 * planes):
                        got = pair[j // planes][f, j % planes, c]
                        turn = (j * width + (width if right else 0)) % count
                        got = pltpu.roll(got, turn, 1) if turn else got
                        side = got if j == 0 else jnp.where(lanes >= j * width, got, side)
                    out[f, c, strip, :] = side

    for lower in (False, True):
        for right in (False, True):
            pl.when(((me >= 2) == lower) & ((even == first) == right))(
                lambda lower=lower, right=right: pack(lower, right)
            )


def beside_tile(right, right_turn, left, left_turn, width):
    lanes = lane_ids(right.shape)
    right = pltpu.roll(right, right_turn, 1) if right_turn else right
    left = pltpu.roll(left, left_turn, 1) if left_turn else left
    return jnp.where(lanes < width, right, jnp.where(lanes >= LANES - width, left, 0.0))


def edge_lanes(shape, margin):
    lanes = lane_ids(shape)
    return (lanes < margin) | (lanes >= LANES - margin)


def slot_lanes(shape, block):
    return lax.rem(lane_ids(shape) + (LANES - 16 * block - LANES // 2 + 8), LANES // 2) < 16


def folded_edges(field, at):
    real, imag = field[at, 0, :, LANES:], field[at, 1, :, LANES:]
    return jnp.where(edge_lanes(real.shape, WIDE), real, pltpu.roll(imag, LANES // 2, 1))


def pack_sides(field, at, out):
    packed = folded_edges(field, at)
    lanes = lane_ids(packed.shape)
    for c, gap in enumerate((DOWN, DOWN + LANES // 2)):
        centre = field[at, c, :, :LANES]
        near, far = pltpu.roll(centre, gap, 1), pltpu.roll(centre, gap + 2 * REACH, 1)
        packed = jnp.where((lanes >= gap) & (lanes < gap + REACH), near, packed)
        packed = jnp.where((lanes >= gap + REACH) & (lanes < gap + 2 * REACH), far, packed)
    out[...] = packed


def unpack_sides(centre, sides, out):
    packed = sides[...]
    lanes = lane_ids(packed.shape)
    keep = edge_lanes(packed.shape, DOWN)
    for c, gap in enumerate((DOWN, DOWN + LANES // 2)):
        near = pltpu.roll(packed, LANES - gap, 1)
        far = pltpu.roll(packed, LANES - gap - 2 * REACH, 1)
        out[c, :, :LANES] = jnp.where(
            lanes < REACH, near, jnp.where(lanes >= LANES - REACH, far, centre[c])
        )
        edges = pltpu.roll(packed, LANES // 2, 1) if c else packed
        out[c, :, LANES:] = jnp.where(keep, edges, 0.0)


def pack_carry(field, at, out):
    rows = field.shape[2]
    out[:rows] = field[at, 0, :, :LANES]
    out[rows : 2 * rows] = field[at, 1, :, :LANES]
    edges = folded_edges(field, at)
    part = rows // 4
    packed = edges[:part]
    for b in range(1, 4):
        turned = pltpu.roll(edges[b * part : (b + 1) * part], 16 * b, 1)
        packed = jnp.where(slot_lanes(packed.shape, b), turned, packed)
    out[2 * rows :] = packed


def unpack_carry(packed, out):
    rows = out.shape[1]
    quarter = packed[2 * rows :]
    edges = jnp.concatenate(
        [pltpu.roll(quarter, LANES - 16 * b, 1) if b else quarter for b in range(4)], axis=0
    )
    keep = edge_lanes(edges.shape, 8)
    for c in range(2):
        out[c, :, :LANES] = packed[c * rows : (c + 1) * rows]
        out[c, :, LANES:] = jnp.where(keep, pltpu.roll(edges, LANES // 2, 1) if c else edges, 0.0)


def times(a, b, q_real, q_imag, sign):
    if sign > 0:
        return a * q_real - b * q_imag, a * q_imag + b * q_real
    return a * q_real + b * q_imag, b * q_real - a * q_imag


def beside_each_other(refs):
    def read(z, c, strip):
        parts = [ref[z, c, strip, :] for ref in refs]
        return parts[0] if len(parts) == 1 else jnp.concatenate(parts, axis=1)

    return read


def difference(one, two):
    return lambda z, c, strip: one[z, c, strip, :] - two[z, c, strip, :]


def sweep(drive, inverse, out, carry, work, planes, rows, reverse):
    drive = drive if callable(drive) else beside_each_other(drive)
    inverse = beside_each_other(inverse)
    rhs, ping, pong = work
    sign = -1 if reverse else 1
    width = out.shape[-1]
    zeros = jnp.zeros((8, width), F32)
    for buffer in (ping, pong):
        for c in range(2):
            buffer[c, :8, :] = zeros
            buffer[c, rows + 8 : rows + 16, :] = zeros

    def beside(buffer, c, r):
        here = buffer[c, r + 8 : r + 24, :]
        return (
            buffer[c, r + 7 : r + 23, :]
            + buffer[c, r + 9 : r + 25, :]
            + (pltpu.roll(here, 1, 1) + pltpu.roll(here, width - 1, 1))
        )

    def plane(step, _):
        z = planes - 1 - step if reverse else step
        for r in range(0, rows, 16):
            strip = slice(r, r + 16)
            a = drive(z, 0, strip) + 2.5 * carry[0, strip, :]
            b = drive(z, 1, strip) + 2.5 * carry[1, strip, :]
            rhs[0, strip, :] = a
            rhs[1, strip, :] = b
            a, b = times(a, b, inverse(z, 0, strip), inverse(z, 1, strip), sign)
            ping[0, r + 8 : r + 24, :] = a
            ping[1, r + 8 : r + 24, :] = b
        for r in range(0, rows, 16):
            strip = slice(r, r + 16)
            a = rhs[0, strip, :] + beside(ping, 0, r)
            b = rhs[1, strip, :] + beside(ping, 1, r)
            a, b = times(a, b, inverse(z, 0, strip), inverse(z, 1, strip), sign)
            pong[0, r + 8 : r + 24, :] = a
            pong[1, r + 8 : r + 24, :] = b
        for r in range(0, rows, 16):
            strip = slice(r, r + 16)
            a = rhs[0, strip, :] + beside(pong, 0, r)
            b = rhs[1, strip, :] + beside(pong, 1, r)
            a, b = times(a, b, inverse(z, 0, strip), inverse(z, 1, strip), sign)
            out[z, 0, strip, :] = a
            out[z, 1, strip, :] = b
            carry[0, strip, :] = a
            carry[1, strip, :] = b
        return 0

    lax.fori_loop(0, planes, plane, 0, unroll=True)


def sweep_scratch(rows, wide=2 * LANES):
    return [
        VMEM((2, rows, wide), F32),
        VMEM((2, rows, wide), F32),
        VMEM((2, rows + 16, wide), F32),
        VMEM((2, rows + 16, wide), F32),
    ]


def inverses(wavenumber, damping):
    real_diag = 6.0 - wavenumber
    denom = real_diag * real_diag + damping * damping
    return jnp.stack([real_diag / denom, -(damping / denom)], axis=1)


def edges_kernel(first, meta, *refs):
    pack_edges(meta, refs[MEMBERS - 1 :: -1], WIDE, first, refs[-1])


def merge_kernel(meta, *refs):
    merge_members(meta, refs[MEMBERS - 1 :: -1], refs[MEMBERS])


def prepare_kernel(ks, meta, source, inverse, *refs):
    for k, send in zip(ks, refs[-len(ks) :]):
        send[0] = source[:, :, meta[0] ^ k]
        send[1] = inverse[...]


def observed_edges_kernel(meta, observed, first, second):
    even = meta[1] == 0
    planes, _, shots, rows, count = observed.shape
    lanes = lane_ids((rows, count))
    per_tile = count // NARROW
    sides = {}
    for s in range(shots):
        for p in range(planes):
            for c in range(2):
                tile, j = divmod((s * planes + p) * 2 + c, per_tile)
                at = j * NARROW
                block = observed[p, c, s]
                for side, turn in (("left", at), ("right", (at + NARROW) % count)):
                    got = pltpu.roll(block, turn, 1) if turn else block
                    if j:
                        got = jnp.where(lanes >= at, got, sides[side])
                    sides[side] = got
                if j == per_tile - 1:
                    first[tile] = jnp.where(even, sides["right"], sides["left"])
                    second[tile] = jnp.where(even, sides["left"], sides["right"])


def observed_sends_kernel(ks, meta, observed, first, second, *refs):
    even = meta[1] == 0
    planes, _, _, rows, count = observed.shape
    lanes = lane_ids((rows, count))
    for k, send in zip(ks, refs[-len(ks) :]):
        shot = meta[0] ^ k
        for p in range(planes):
            for c in range(2):
                send[2 * p + c] = observed[p, c, shot]
        one, two = first[shot // 2], second[shot // 2]
        right, left = jnp.where(even, one, two), jnp.where(even, two, one)
        odd = lax.rem(shot, 2)
        right = pltpu.roll(right, odd * (count // 2), 1)
        left = pltpu.roll(left, (1 - odd) * (count // 2), 1)
        send[2 * planes] = jnp.where(lanes < count // 2, right, left)


def merge_observed_kernel(meta, *refs):
    pieces, out = refs[MEMBERS - 1 :: -1], refs[-1]
    planes = out.shape[0] // 2
    _, rows, count = pieces[0].shape
    for k, piece in enumerate(pieces):
        who = meta[0] ^ k
        at_plane = (who // 2) * planes
        strip = pl.ds(pl.multiple_of((who % 2) * rows, rows), rows)
        edges = piece[2 * planes]
        for p in range(planes):
            for c in range(2):
                at = (2 * p + c) * NARROW
                out[at_plane + p, c, strip, :LANES] = piece[2 * p + c]
                out[at_plane + p, c, strip, LANES:] = beside_tile(
                    edges,
                    (count - at) % count,
                    edges,
                    (count // 2 - NARROW - at) % count,
                    NARROW,
                )


def centre_kernel(meta, merged, send, field, carry, *work):
    planes, rows = merged.shape[1], merged.shape[3]

    @pl.when(meta[2] == 0)
    def _():
        carry[...] = jnp.zeros_like(carry)
        sweep([merged.at[0]], [merged.at[1]], field, carry, work, planes, rows, False)
        send[...] = carry[...]


def forward_kernel(meta, merged, second, first, sides, field, send, carry, *work):
    planes, rows = merged.shape[1], merged.shape[3]
    even, alone = meta[1] == 0, meta[3]
    for f in range(2):
        for c in range(2):
            for r in range(0, rows, 32):
                strip = slice(r, r + 32)
                one, two = first[f, c, strip, :], second[f, c, strip, :]
                two = jnp.where(alone, 0.0, two) if f else two
                right, left = jnp.where(even, one, two), jnp.where(even, two, one)
                for p in range(planes):
                    at = p * WIDE
                    sides[f, p, c, strip, :] = beside_tile(
                        right, (LANES - at) % LANES, left, (2 * LANES - WIDE - at) % LANES, WIDE
                    )

    @pl.when(meta[2] == 0)
    def _():
        carry[...] = jnp.zeros_like(carry)
        drive, inverse = ([merged.at[f], sides.at[f]] for f in range(2))
        sweep(drive, inverse, field, carry, work, planes, rows, False)
        pack_sides(field, planes - 1, send)


def cut_kernel(height, meta, field, _, *pieces):
    planes, rows = field.shape[0], field.shape[2]
    margin = (rows - 2 * height) // 2
    for k, piece in enumerate(pieces):
        who = meta[0] ^ k
        at_plane = (who // 2) * (planes // 2)
        at_row = pl.multiple_of((who % 2) * height + margin, 8)
        for p in range(planes // 2):
            for c in range(2):
                piece[p, c] = field[at_plane + p, c, pl.ds(at_row, height), :LANES]


def turn_kernel(
    meta,
    merged,
    beside,
    centre,
    sides,
    observed,
    upper_field,
    field,
    adjoint,
    send,
    carry,
    *work,
):
    planes, rows = merged.shape[1], merged.shape[3]
    drive, inverse = ([merged.at[f], beside.at[f]] for f in range(2))
    lower = meta[2] == 1

    @pl.when(jnp.logical_not(lower))
    def _():
        field[...] = upper_field[...]

    @pl.when(lower)
    def _():
        unpack_sides(centre, sides, carry)
        sweep(drive, inverse, field, carry, work, planes, rows, False)
        carry[...] = jnp.zeros_like(carry)
        sweep(difference(field, observed), inverse, adjoint, carry, work, planes, rows, True)
        pack_carry(adjoint, 0, send)


def adjoint_kernel(height, meta, observed, merged, beside, got, field, lower_adjoint, *rest):
    pieces, (adjoint, carry, *work) = rest[:MEMBERS], rest[MEMBERS:]
    planes, rows = field.shape[0], field.shape[2]
    margin = (rows - 2 * height) // 2
    upper = meta[2] == 0
    inverse = [merged.at[1], beside.at[1]]

    def products(adjoint):
        for k, piece in enumerate(pieces):
            who = meta[0] ^ k
            at_plane = (who // 2) * (planes // 2)
            at_row = pl.multiple_of((who % 2) * height + margin, 8)
            for p in range(planes // 2):
                total = 0.0
                for c in range(2):
                    total += (
                        field[at_plane + p, c, pl.ds(at_row, height), :LANES]
                        * adjoint[at_plane + p, c, pl.ds(at_row, height), :LANES]
                    )
                piece[p] = total * (1.0 / MEMBERS)

    @pl.when(upper)
    def _():
        unpack_carry(got, carry)
        sweep(difference(field, observed), inverse, adjoint, carry, work, planes, rows, True)
        products(adjoint)

    @pl.when(jnp.logical_not(upper))
    def _():
        products(lower_adjoint)


def sum_kernel(meta, one, two, three, four, out):
    out[...] = (one[...] + two[...]) + (three[...] + four[...])


def field_kernel(meta, *refs):
    out = refs[MEMBERS]
    for k, piece in enumerate(refs[MEMBERS - 1 :: -1]):
        out[:, :, meta[0] ^ k] = piece[...]


def body(source, observed, wavenumber, damping):
    own_planes, _, shots, height, width = source.shape
    planes, high = 2 * own_planes, 2 * height
    one_group = lax.axis_size("gx") == 2
    rows = high if one_group else high + 2 * WIDE
    tile = (own_planes, 2, height, width)

    inverse = inverses(wavenumber, damping)
    far = call(
        lambda *refs: prepare_kernel(ACROSS, *refs), [(2, *tile)] * 2, source, inverse
    )
    near = call(
        lambda *refs: prepare_kernel(ALONG, *refs), [(2, *tile)] * 2, source, inverse, far[0]
    )
    sends = [*near, *far]
    observed, *sends = lax.optimization_barrier([observed, *sends])
    pieces = gathered(sends)
    seen_edges = call(observed_edges_kernel, [(2, height, width)] * 2, observed)
    seen_edges = side_swaps(*seen_edges)
    *pieces, one, two = lax.optimization_barrier([*pieces, *seen_edges])
    edge_shape = (2, 2, high, width)
    (second,) = call(lambda *refs: edges_kernel(False, *refs), [edge_shape], *pieces)
    (merged,) = call(merge_kernel, [(2, planes, 2, high, width)], *pieces)
    if not one_group:
        merged = with_row_halo(merged, WIDE)
    (centre,) = call(
        centre_kernel,
        [(2, rows, width)],
        merged,
        scratch=[VMEM((planes, 2, rows, width), F32), *sweep_scratch(rows, width)],
    )
    (first,) = call(lambda *refs: edges_kernel(True, *refs), [edge_shape], *pieces, centre)
    packed = first
    if not one_group:
        first, second = (with_row_halo(a, WIDE) for a in (first, second))
    first, second = side_swaps(first, second)
    centre = depth_pair_swap(centre)
    shape = [(2 * own_planes + 1, height, width)] * 2
    far = call(lambda *refs: observed_sends_kernel(ACROSS, *refs), shape, observed, one, two, packed)
    near = call(
        lambda *refs: observed_sends_kernel(ALONG, *refs), shape, observed, one, two, far[0]
    )
    seen = gathered([*near, *far])

    whole = (planes, 2, rows, 2 * width)
    scratch = sweep_scratch(rows)
    beside, field, send = call(
        forward_kernel,
        [(2, planes, 2, rows, width), whole, (rows, width)],
        merged,
        second,
        first,
        scratch=scratch,
        cost=30_000_000,
    )
    got = depth_pair_swap(send)
    (seen,) = call(
        merge_observed_kernel, [(planes, 2, high, 2 * width)], *seen, centre, cost=3_000_000
    )
    seen = seen if one_group else with_row_halo(seen, WIDE)
    field, adjoint, send = call(
        turn_kernel,
        [whole, whole, (2 * rows + rows // 4, width)],
        merged,
        beside,
        centre,
        got,
        seen,
        field,
        scratch=scratch,
    )
    got = depth_pair_swap(send)
    pieces = gathered(
        call(lambda *refs: cut_kernel(height, *refs), [tile] * MEMBERS, field, send)
    )
    sums = call(
        lambda *refs: adjoint_kernel(height, *refs),
        [(own_planes, height, width)] * MEMBERS,
        seen,
        merged,
        beside,
        got,
        field,
        adjoint,
        scratch=[VMEM(whole, F32), *scratch],
    )
    sums = gathered(sums)
    (gradient,) = call(sum_kernel, [wavenumber.shape], *sums)
    (forward_field,) = call(field_kernel, [source.shape], *pieces)
    return forward_field, gradient


def solution(mesh):
    lateral = P("depth", None, None, "gx", "gy")
    return jax.shard_map(
        body,
        mesh=mesh,
        in_specs=(lateral, lateral, P("depth", "gx", "gy"), P("depth", "gx", "gy")),
        out_specs=(lateral, P("depth", "gx", "gy")),
        check_vma=False,
    )
```
